128 devices in a mesh: ta: 4 (over y_hi, core), gy: 32 (over y_lo, z, x).
Axes of the slice: x: 4, y: 4 (y_hi: 2, y_lo: 2; y = y_hi * 2 + y_lo), z: 4, core: 2. Of those that a mesh axis runs over, the one named last changes fastest.
Arguments:
- charge_field: bfloat16 [32, 2048, 2048], P('ta', 'gy'), may hold values from -324 to 324
Outputs:
- spectrum: float32 [32, 2048, 2048], P(None, 'gy', 'ta')
The draws below stay inside these ranges and needn't reach their ends.
All inputs are finite; a program needn't handle non-finite values.
Results may differ from the reference program's by a relative error of at most 0.023.
Values may be sent and summed in bfloat16 or wider, within the bound.
A program may use at most 128 MiB of HBM per device.

```python
import math
import jax
import jax.numpy as jnp
from jax import lax

FR = 32
NX = 2048
NY = 2048
PX = 32
PY = 32


def draw_charge_field(key, part):
    key = jax.random.fold_in(key, 7)
    frames = jnp.arange(FR, dtype=jnp.int32)
    nearest = jnp.minimum(frames, FR - 1 - frames).astype(jnp.float32)
    envelope = 1.0 + 80.0 * jnp.exp(-nearest)
    values = jnp.clip(jax.random.normal(key, (FR, NY, NX), jnp.float32), -4.0, 4.0)
    return (values * envelope[:, None, None]).astype(jnp.bfloat16)


def setup_inputs(seed: int = 0) -> dict:
    seeds = jax.random.split(jax.random.key(seed), 2)
    charge_field = draw_charge_field(jax.random.fold_in(seeds[1], 71), 0)
    return dict(charge_field=charge_field)


def dft_tables(length, rows_idx, cols_idx):
    phases = (rows_idx[:, None] * cols_idx[None, :]) % length
    angles = phases.astype(jnp.float32) * (2.0 * math.pi / length)
    return jnp.cos(angles).astype(jnp.bfloat16), jnp.sin(angles).astype(jnp.bfloat16)


def time_tables(count):
    places = jnp.arange(count, dtype=jnp.int32)
    phases = (places[:, None] * places[None, :]) % count
    angles = phases.astype(jnp.float32) * (2.0 * math.pi / count)
    window = 0.5 - 0.5 * jnp.cos((places.astype(jnp.float32) + 0.5) * (2.0 * math.pi / count))
    cos_w = (jnp.cos(angles) * window[None, :]).astype(jnp.bfloat16)
    sin_w = (jnp.sin(angles) * window[None, :]).astype(jnp.bfloat16)
    return cos_w, sin_w, jnp.sum(window * window)


def rounded(values):
    return values.astype(jnp.bfloat16).astype(jnp.float32)


def factored(real_in, imag_in, first):
    highest = lax.Precision.HIGHEST
    rows, length = real_in.shape
    second = length // first
    idx_a = jnp.arange(first, dtype=jnp.int32)
    idx_b = jnp.arange(second, dtype=jnp.int32)
    cos_a, sin_a = dft_tables(first, idx_a, idx_a)
    cos_b, sin_b = dft_tables(second, idx_b, idx_b)
    cos_t, sin_t = dft_tables(length, idx_a, idx_b)
    cos_a = cos_a.astype(jnp.float32)
    sin_a = sin_a.astype(jnp.float32)
    cos_b = cos_b.astype(jnp.float32)
    sin_b = sin_b.astype(jnp.float32)
    cos_t = cos_t.astype(jnp.float32)
    sin_t = sin_t.astype(jnp.float32)
    real_r = real_in.astype(jnp.float32).reshape(rows, first, second)
    first_real = jnp.einsum("rab,ak->rkb", real_r, cos_a, precision=highest)
    first_imag = -jnp.einsum("rab,ak->rkb", real_r, sin_a, precision=highest)
    if imag_in is not None:
        imag_r = imag_in.astype(jnp.float32).reshape(rows, first, second)
        first_real = first_real + jnp.einsum("rab,ak->rkb", imag_r, sin_a, precision=highest)
        first_imag = first_imag + jnp.einsum("rab,ak->rkb", imag_r, cos_a, precision=highest)
    first_real = rounded(first_real)
    first_imag = rounded(first_imag)
    turn_real = rounded(first_real * cos_t + first_imag * sin_t)
    turn_imag = rounded(first_imag * cos_t - first_real * sin_t)
    out_real = jnp.einsum("rkn,nm->rmk", turn_real, cos_b, precision=highest) + jnp.einsum("rkn,nm->rmk", turn_imag, sin_b, precision=highest)
    out_imag = jnp.einsum("rkn,nm->rmk", turn_imag, cos_b, precision=highest) - jnp.einsum("rkn,nm->rmk", turn_real, sin_b, precision=highest)
    return out_real.reshape(rows, length).astype(jnp.bfloat16), out_imag.reshape(rows, length).astype(jnp.bfloat16)


def reference(charge_field):
    highest = lax.Precision.HIGHEST

    def one_frame(frame):
        real_x, imag_x = factored(frame, None, PX)
        real_y, imag_y = factored(real_x.T, imag_x.T, PY)
        return jnp.stack([real_y, imag_y])

    spectra = lax.map(one_frame, charge_field)
    cos_b, sin_b, wsum = time_tables(FR)
    cos_t = cos_b.astype(jnp.float32)
    sin_t = sin_b.astype(jnp.float32)
    scale_total = NX * NY * wsum
    width = min(512, NX)

    def time_block(start):
        piece_all = lax.dynamic_slice_in_dim(spectra, start, width, 2).astype(jnp.float32)
        real_in = piece_all[:, 0]
        imag_in = piece_all[:, 1]
        real_t = jnp.einsum("wt,txk->wxk", cos_t, real_in, precision=highest) + jnp.einsum("wt,txk->wxk", sin_t, imag_in, precision=highest)
        imag_t = jnp.einsum("wt,txk->wxk", cos_t, imag_in, precision=highest) - jnp.einsum("wt,txk->wxk", sin_t, real_in, precision=highest)
        return (real_t * real_t + imag_t * imag_t) / scale_total

    starts = (jnp.arange(NX // width, dtype=jnp.int32) * width).astype(jnp.int32)
    blocks = lax.map(time_block, starts)
    return jnp.transpose(blocks, (1, 0, 2, 3)).reshape(FR, NX, NY)
```

```python
import functools
import math

import jax
import jax.numpy as jnp
import ml_dtypes
import numpy as np
from jax import lax
from jax.experimental import pallas as pl
from jax.experimental.pallas import tpu as pltpu
from jax.sharding import PartitionSpec as P

FR, NX, NY = 32, 2048, 2048
TA, GY = 4, 32
DEV = TA * GY
FT = FR // TA
YL = NY // GY
SLOT = 8
HALF = GY // 2
F32, BF16 = jnp.float32, jnp.bfloat16
MIB = 1 << 20


def bf(a):
    return np.asarray(a).astype(np.float32).astype(ml_dtypes.bfloat16)


def device_of(group, part):
    a, h = part % TA, part // TA
    return a * GY + (group if h == 0 else GY - 1 - group)


@functools.lru_cache(None)
def x_tables():
    kx = np.zeros((2, DEV, 4), np.int64)
    for group in range(HALF):
        for part in range(8):
            for parity in range(2):
                base = 64 * group + 8 * part + parity
                kx[parity, device_of(group, part)] = base + 2 * np.arange(4)
    n = np.arange(NX // 2)
    angle = 2 * np.pi * ((kx[..., None] * n) % NX) / NX
    re, im = np.cos(angle), -np.sin(angle)
    zero = device_of(0, 0)
    im[0, zero, 0] = np.cos(np.pi * n)
    both = np.stack([re, im], axis=2)
    return bf(both.reshape(2, DEV * 8, NX // 2))


@functools.lru_cache(None)
def t_table():
    t = np.arange(FR)
    window = 0.5 - 0.5 * np.cos(2 * np.pi * (t + 0.5) / FR)
    angle = 2 * np.pi * ((t[:, None] * t[None, :]) % FR) / FR
    cw, sw = np.cos(angle) * window, np.sin(angle) * window
    out = np.zeros((2, 4, FR, FR, 2, 4))
    for p in range(4):
        out[0, p, :, :, 0, p] = cw
        out[0, p, :, :, 1, p] = sw
        out[1, p, :, :, 0, p] = -sw
        out[1, p, :, :, 1, p] = cw
    extra = np.zeros((2, FR, FR, 2, 4))
    extra[0, :, :, 1, 0] = cw
    extra[1, :, :, 1, 0] = -sw
    k = FR * 8
    return bf(np.concatenate([out.reshape(k, k), extra.reshape(2 * FR, k)])), float(np.sum(window * window))


@functools.lru_cache(None)
def y_tables():
    n, k = np.arange(NY // 4), np.arange(NY // 4)
    out = []
    for q in (0, 2, 1):
        angle = 2 * np.pi * ((n[:, None] * (4 * k[None, :] + q)) % NY) / NY
        cs = np.stack([np.cos(angle).reshape(-1, 4, 128), np.sin(angle).reshape(-1, 4, 128)], axis=2)
        out.append(cs.transpose(1, 0, 2, 3).reshape(4, NY // 4, 256))
    return bf(np.stack(out))


@functools.lru_cache(None)
def row_tables():
    direct = np.zeros((FR, 8, 2, 4, FR))
    mirror = np.zeros((FR, 8, 2, 4, FR))
    corner = np.zeros((FR, 2, 4, FR))
    for w in range(FR):
        for j in range(8):
            direct[w, j, j % 2, j // 2, w] = 1
            mirror[w, (8 - j) % 8, j % 2, j // 2, -w % FR] = 1
        corner[w, 0, 0, -w % FR] = 1
    k = FR * 8
    return bf(direct.reshape(k, k)), bf(np.concatenate([mirror.reshape(k, k), corner.reshape(FR, k)]))


@functools.lru_cache(None)
def ky_table():
    out = np.zeros((4, 128, 128, 4))
    k = np.arange(128)
    for q in range(3):
        out[q, k, k, q] = 1
    out[3, k, 127 - k, 3] = 1
    return bf(out.reshape(512, 512))


def halves(first, second):
    low = lax.broadcasted_iota(jnp.int32, first.shape, first.ndim - 1) < 64
    one = jnp.where(low, first, pltpu.roll(second, 64, first.ndim - 1))
    two = jnp.where(low, pltpu.roll(first, 64, first.ndim - 1), second)
    return one, two


NT = (((1,), (1,)), ((), ()))
X_STEPS = 4
X_ROWS = DEV * 8 // X_STEPS


def x_kernel(field, table, out, even, odd):
    @pl.when(pl.program_id(0) == 0)
    def _():
        for t in range(FT):
            lo = field[t, :, : NX // 2].astype(F32)
            hi = field[t, :, NX // 2 :].astype(F32)
            even[YL * t : YL * (t + 1)] = (lo + hi).astype(BF16)
            odd[YL * t : YL * (t + 1)] = (lo - hi).astype(BF16)

    for s in range(2):
        for r in range(0, X_ROWS, 128):
            rows = slice(r, r + 128)
            e = lax.dot_general(table[0, rows], even[256 * s : 256 * (s + 1)], NT, preferred_element_type=F32)
            o = lax.dot_general(table[1, rows], odd[256 * s : 256 * (s + 1)], NT, preferred_element_type=F32)
            for q in range(2):
                lanes = slice(128 * q, 128 * (q + 1))
                one, two = halves(e[:, lanes], o[:, lanes])
                both = jnp.concatenate([one.reshape(16, 8, 128), two.reshape(16, 8, 128)], axis=1)
                at = 16 * (2 * s + q)
                out[r // 8 : r // 8 + 16, at : at + 16] = both.astype(BF16)


def x_transform(field, table):
    return pl.pallas_call(
        x_kernel,
        grid=(X_STEPS,),
        out_shape=jax.ShapeDtypeStruct((DEV, 8 * FT, 128), BF16),
        in_specs=[
            pl.BlockSpec((FT, YL, NX), lambda s: (0, 0, 0)),
            pl.BlockSpec((2, X_ROWS, NX // 2), lambda s: (0, s, 0)),
        ],
        out_specs=pl.BlockSpec((DEV // X_STEPS, 8 * FT, 128), lambda s: (s, 0, 0)),
        scratch_shapes=[pltpu.VMEM((FT * YL, NX // 2), BF16)] * 2,
        compiler_params=pltpu.CompilerParams(vmem_limit_bytes=48 * MIB),
        name="x_transform",
    )(field, table)


def yt_kernel(scale, rec, tt, ty, rows_d, rows_m, out, corner, u0, u1, u2, u3, power_d, power_m):
    special = (lax.axis_index("ta") == 0) & (lax.axis_index("gy") == 0)
    flag = jnp.where(special, 1.0, 0.0).astype(F32)

    def time_step(q, carry):
        z = []
        for n in range(4):
            pair = 4 * n + q
            left = rec[:, 2 * pair].reshape(256, 128)
            right = rec[:, 2 * pair + 1].reshape(256, 128)
            v = jnp.dot(tt[...], jnp.concatenate([left, right], axis=1), preferred_element_type=F32)
            ve, vo = halves(v[:, :128], v[:, 128:])
            re0 = ve[:32] + flag * ve[288:320]
            im0 = ve[128:160] - flag * ve[256:288]
            re = jnp.concatenate([re0, ve[32:128], vo[:128], ve[256:288]], axis=0)
            im = jnp.concatenate([im0, ve[160:256], vo[128:256], ve[288:320]], axis=0)
            z.append((re, im))
        (ar, ai), (br, bi), (cr, ci), (dr, di) = z
        sr, si, tr, ti = ar + cr, ai + ci, br + dr, bi + di
        er, ei, fr, fi = ar - cr, ai - ci, br - dr, bi - di
        lanes = pl.ds(pl.multiple_of(128 * q, 128), 128)
        for ref, re, im in (
            (u0, sr + tr, si + ti),
            (u1, er + fi, ei - fr),
            (u2, sr - tr, si - ti),
            (u3, er - fi, ei + fr),
        ):
            ref[:288, lanes] = re.astype(BF16)
            ref[288:, lanes] = im.astype(BF16)
        return carry

    lax.fori_loop(0, 4, time_step, 0)

    def products(ref, table):
        both = jnp.dot(ref[...], table, preferred_element_type=F32)
        return both[:288, :128], both[:288, 128:], both[288:, :128], both[288:, 128:]

    def plus(p1, p2, p3, p4):
        re, im = p1 + p4, p3 - p2
        return (re * re + im * im) * scale

    def minus(p1, p2, p3, p4):
        re, im = p1 - p4, p3 + p2
        return (re * re + im * im) * scale

    def y_step(a, carry):
        def put(ref, block, quarter, value):
            lanes = pl.ds(pl.multiple_of(512 * block + 128 * quarter, 128), 128)
            ref[:, lanes] = value.astype(BF16)

        def mirrored(value):
            return jnp.concatenate([jnp.where(special, value[256:], value[:32]), value[32:256]], axis=0)

        for c, ref in ((0, u0), (2, u2)):
            parts = products(ref, ty[c // 2, a])
            put(power_d, a, c, plus(*parts)[:256])
            put(power_m, a, c, mirrored(minus(*parts)))
        up = plus(*products(u1, ty[2, a]))
        put(power_d, a, 1, up[:256])
        put(power_m, 3 - a, 3, mirrored(up))
        down = minus(*products(u3, ty[2, a]))
        put(power_m, a, 1, mirrored(down))
        put(power_d, 3 - a, 3, down[:256])
        return carry

    lax.fori_loop(0, 4, y_step, 0)

    def row_step(a, carry):
        lanes = pl.ds(pl.multiple_of(512 * a, 512), 512)
        out[a] = jnp.dot(rows_d[...], power_d[:, lanes], preferred_element_type=F32).astype(BF16)
        both = jnp.dot(rows_m[...], power_m[:, lanes], preferred_element_type=F32).astype(BF16)
        out[4 + a] = both[:256]
        corner[a] = both[256:]
        return carry

    lax.fori_loop(0, 4, row_step, 0)


def yt_transform(rec, tt, ty, rows_d, rows_m, scale):
    vm = pl.BlockSpec(memory_space=pltpu.VMEM)
    return pl.pallas_call(
        functools.partial(yt_kernel, scale),
        out_shape=(
            jax.ShapeDtypeStruct((8, 256, 512), BF16),
            jax.ShapeDtypeStruct((4, 32, 512), BF16),
        ),
        in_specs=[vm] * 5,
        out_specs=(vm, vm),
        scratch_shapes=[pltpu.VMEM((576, 512), BF16)] * 4 + [pltpu.VMEM((256, 2048), BF16)] * 2,
        compiler_params=pltpu.CompilerParams(vmem_limit_bytes=56 * MIB),
        name="yt_transform",
    )(rec, tt, ty, rows_d, rows_m)


def spread_kernel(blocks, corner, out, corner_out, send, recv, local, corner_send, corner_recv):
    a, g = lax.axis_index("ta"), lax.axis_index("gy")
    h = g // HALF
    group = jnp.where(h == 0, g, GY - 1 - g)
    part = a + TA * h

    def target(member):
        ta, th = member % TA, member // TA
        return ta, jnp.where(th == 0, group, GY - 1 - group), th

    slot_here = jnp.where(h == 0, part, 7 - part)
    own = pltpu.make_async_copy(blocks.at[part], out.at[slot_here], local)
    own.start()

    def send_one(k, carry):
        member = (part + k) % 8
        ta, tg, th = target(member)
        slot = jnp.where(th == 0, part, 7 - part)
        pltpu.make_async_remote_copy(
            src_ref=blocks.at[member],
            dst_ref=out.at[slot],
            send_sem=send,
            recv_sem=recv,
            device_id=(ta, tg),
            device_id_type=pl.DeviceIdType.MESH,
        ).start()
        return carry

    lax.fori_loop(1, 8, send_one, 0)
    has_corner = part == 0
    corner_to = GY - 1 - (group + HALF - 1) % HALF

    @pl.when(has_corner)
    def _():
        for ta in range(TA):
            pltpu.make_async_remote_copy(
                src_ref=corner.at[ta],
                dst_ref=corner_out,
                send_sem=corner_send,
                recv_sem=corner_recv,
                device_id=(ta, corner_to),
                device_id_type=pl.DeviceIdType.MESH,
            ).start()
        pltpu.make_async_copy(corner, corner, corner_send).wait()

    @pl.when(h == 1)
    def _():
        pltpu.make_async_copy(corner_out, corner_out, corner_recv).wait()

    own.wait()
    seven = out.at[pl.ds(0, 7)]
    pltpu.make_async_copy(seven, seven, recv).wait()
    pltpu.make_async_copy(seven, seven, send).wait()


def spread(blocks, corner):
    anywhere = pl.BlockSpec(memory_space=pl.ANY)
    return pl.pallas_call(
        spread_kernel,
        out_shape=(
            jax.ShapeDtypeStruct((8, 256, 512), BF16),
            jax.ShapeDtypeStruct((32, 512), BF16),
        ),
        in_specs=[anywhere] * 2,
        out_specs=(anywhere, anywhere),
        scratch_shapes=[pltpu.SemaphoreType.DMA] * 5,
        compiler_params=pltpu.CompilerParams(has_side_effects=True),
        name="spread",
    )(blocks, corner)


def last_kernel(block, below, corner, order, out):
    m = pl.program_id(0)
    mirrored = lax.axis_index("gy") >= HALF
    here = jnp.dot(block[0], order[...], preferred_element_type=F32).reshape(FR, 8, 512)
    out[...] = here

    @pl.when(mirrored)
    def _():
        low = jnp.dot(below[0], order[...], preferred_element_type=F32).reshape(FR, 8, 512)
        first = lax.broadcasted_iota(jnp.int32, (FR, 8, 512), 1) == 0
        out[...] = jnp.where(first, low, here)

        @pl.when(m == 0)
        def _():
            edge = jnp.dot(corner[...], order[...], preferred_element_type=F32)
            out[:, 0:1, :] = edge.reshape(FR, 1, 512)


def last_step(blocks, corner, order):
    return pl.pallas_call(
        last_kernel,
        grid=(8,),
        out_shape=jax.ShapeDtypeStruct((FR, 64, 512), F32),
        in_specs=[
            pl.BlockSpec((1, 256, 512), lambda m: (m, 0, 0)),
            pl.BlockSpec((1, 256, 512), lambda m: (jnp.maximum(m - 1, 0), 0, 0)),
            pl.BlockSpec((32, 512), lambda m: (0, 0)),
            pl.BlockSpec((512, 512), lambda m: (0, 0)),
        ],
        out_specs=pl.BlockSpec((FR, 8, 512), lambda m: (0, m, 0)),
        compiler_params=pltpu.CompilerParams(vmem_limit_bytes=32 * MIB),
        name="last_step",
    )(blocks, blocks, corner, order)


def shards(charge_field):
    tt, wsum = t_table()
    rows_d, rows_m = row_tables()
    slots = x_transform(charge_field, jnp.asarray(x_tables()))
    rec = lax.all_to_all(slots, ("ta", "gy"), 0, 0)
    rec = rec.reshape(TA, GY, 8 * FT, 128)
    blocks, corner = yt_transform(
        rec, jnp.asarray(tt), jnp.asarray(y_tables()), jnp.asarray(rows_d), jnp.asarray(rows_m), 1.0 / (NX * NY * wsum)
    )
    blocks, corner = spread(blocks, corner)
    return last_step(blocks, corner, jnp.asarray(ky_table()))


def solution(mesh):
    return jax.shard_map(
        shards, mesh=mesh, in_specs=(P("ta", "gy", None),), out_specs=P(None, "gy", "ta"), check_vma=False
    )
```

```python
import functools
import math

import jax
import jax.numpy as jnp
import ml_dtypes
import numpy as np
from jax import lax
from jax.experimental import pallas as pl
from jax.experimental.pallas import tpu as pltpu
from jax.sharding import PartitionSpec as P

FR, NX, NY = 32, 2048, 2048
TA, GY = 4, 32
DEV = TA * GY
FT = FR // TA
YL = NY // GY
SLOT = 8
HALF = GY // 2
F32, BF16 = jnp.float32, jnp.bfloat16
MIB = 1 << 20


def bf(a):
    return np.asarray(a).astype(np.float32).astype(ml_dtypes.bfloat16)


def place(group, part):
    a, h = part % TA, part // TA
    return a, group if h == 0 else GY - 1 - group


def order_of(a, g):
    y, core = 2 * (a // 2) + g // 16, a % 2
    z, x = g // 4 % 4, g % 4
    return ((x + y + z) % 4 * 2 + core) * 16 + 4 * y + x


@functools.lru_cache(None)
def x_tables():
    kx = np.zeros((2, DEV, 4), np.int64)
    for group in range(HALF):
        for part in range(8):
            for parity in range(2):
                base = 64 * group + 8 * part + parity
                kx[parity, order_of(*place(group, part))] = base + 2 * np.arange(4)
    n = np.arange(NX // 2)
    angle = 2 * np.pi * ((kx[..., None] * n) % NX) / NX
    re, im = np.cos(angle), -np.sin(angle)
    zero = order_of(*place(0, 0))
    im[0, zero, 0] = np.cos(np.pi * n)
    both = np.stack([re, im], axis=2)
    return bf(both.reshape(2, DEV * 8, NX // 2))


@functools.lru_cache(None)
def t_table():
    t = np.arange(FR)
    window = 0.5 - 0.5 * np.cos(2 * np.pi * (t + 0.5) / FR)
    angle = 2 * np.pi * ((t[:, None] * t[None, :]) % FR) / FR
    cw, sw = np.cos(angle) * window, np.sin(angle) * window
    out = np.zeros((2, 4, FR, FR, 2, 4))
    for p in range(4):
        out[0, p, :, :, 0, p] = cw
        out[0, p, :, :, 1, p] = sw
        out[1, p, :, :, 0, p] = -sw
        out[1, p, :, :, 1, p] = cw
    extra = np.zeros((2, FR, FR, 2, 4))
    extra[0, :, :, 1, 0] = cw
    extra[1, :, :, 1, 0] = -sw
    k = FR * 8
    return bf(np.concatenate([out.reshape(k, k), extra.reshape(2 * FR, k)])), float(np.sum(window * window))


@functools.lru_cache(None)
def y_tables():
    n, k = np.arange(NY // 4), np.arange(NY // 4)
    out = []
    for q in (0, 2, 1):
        angle = 2 * np.pi * ((n[:, None] * (4 * k[None, :] + q)) % NY) / NY
        cs = np.stack([np.cos(angle).reshape(-1, 4, 128), np.sin(angle).reshape(-1, 4, 128)], axis=2)
        out.append(cs.transpose(1, 0, 2, 3).reshape(4, NY // 4, 256))
    return bf(np.stack(out))


@functools.lru_cache(None)
def row_tables():
    direct = np.zeros((FR, 8, 2, 4, FR))
    mirror = np.zeros((FR, 8, 2, 4, FR))
    corner = np.zeros((FR, 2, 4, FR))
    for w in range(FR):
        for j in range(8):
            direct[w, j, j % 2, j // 2, w] = 1
            mirror[w, (8 - j) % 8, j % 2, j // 2, -w % FR] = 1
        corner[w, 0, 0, -w % FR] = 1
    k = FR * 8
    return bf(direct.reshape(k, k)), bf(np.concatenate([mirror.reshape(k, k), corner.reshape(FR, k)]))


@functools.lru_cache(None)
def ky_table():
    out = np.zeros((4, 128, 128, 4))
    k = np.arange(128)
    for q in range(3):
        out[q, k, k, q] = 1
    out[3, k, 127 - k, 3] = 1
    return bf(out.reshape(512, 512))


def halves(first, second):
    low = lax.broadcasted_iota(jnp.int32, first.shape, first.ndim - 1) < 64
    one = jnp.where(low, first, pltpu.roll(second, 64, first.ndim - 1))
    two = jnp.where(low, pltpu.roll(first, 64, first.ndim - 1), second)
    return one, two


NT = (((1,), (1,)), ((), ()))
MESH = pl.DeviceIdType.MESH
CHUNKS = 8
CHUNK = DEV // CHUNKS


def fused_kernel(
    scale, field_in, xt_in, tt_in, ty_in, rd_in, rm_in, out, corner_out,
    field, xt, tt, ty, rows_d, rows_m, even, odd, slots, rec, u0, u1, u2, u3, power_d, power_m, blocks, corner,
    load, send, recv, local, send2, recv2, local2, corner_send, corner_recv,
):
    a, g = lax.axis_index("ta"), lax.axis_index("gy")
    me = a * GY + g
    my_y, my_core, my_z, my_x = 2 * (a // 2) + g // 16, a % 2, g // 4 % 4, g % 4

    loads = [
        pltpu.make_async_copy(src, dst, load.at[i])
        for i, (src, dst) in enumerate(
            ((field_in, field), (xt_in, xt), (tt_in, tt), (ty_in, ty), (rd_in, rows_d), (rm_in, rows_m))
        )
    ]
    for copy in loads:
        copy.start()

    barrier = pltpu.get_barrier_semaphore()

    def greet(o, carry):
        peer = (me + o) % DEV
        pl.semaphore_signal(barrier, inc=1, device_id=(peer // GY, peer % GY), device_id_type=MESH)
        return carry

    lax.fori_loop(1, DEV, greet, 0)

    loads[0].wait()

    def fold(t, carry):
        rows = pl.ds(pl.multiple_of(YL * t, YL), YL)
        lo = field[t, :, : NX // 2].astype(F32)
        hi = field[t, :, NX // 2 :].astype(F32)
        even[rows] = (lo + hi).astype(BF16)
        odd[rows] = (lo - hi).astype(BF16)
        return carry

    lax.fori_loop(0, FT, fold, 0)
    loads[1].wait()

    first = (my_x + my_y + my_z) % 4 * 2 + my_core

    def x_step(c, carry):
        k = (first + c) % CHUNKS
        rows = pl.ds(pl.multiple_of(128 * k, 128), 128)
        for s in range(2):
            e = lax.dot_general(xt[0, rows], even[256 * s : 256 * (s + 1)], NT, preferred_element_type=F32)
            o = lax.dot_general(xt[1, rows], odd[256 * s : 256 * (s + 1)], NT, preferred_element_type=F32)
            for q in range(2):
                lanes = slice(128 * q, 128 * (q + 1))
                one, two = halves(e[:, lanes], o[:, lanes])
                both = jnp.concatenate([one.reshape(16, 8, 128), two.reshape(16, 8, 128)], axis=1)
                at = 16 * (2 * s + q)
                slots[pl.ds(16 * k, 16), at : at + 16] = both.astype(BF16)

        @pl.when(c == 0)
        def _():
            pl.semaphore_wait(barrier, DEV - 1)

        total, core = k // 2, k % 2

        def send_step(i, carry):
            y, x = (my_y + i // 4) % 4, (my_x + i % 4) % 4
            z = (total + 8 - x - y) % 4
            ta, tg = 2 * (y // 2) + core, 16 * (y % 2) + 4 * z + x
            src = slots.at[16 * k + 4 * y + x]
            dst = rec.at[me]
            mine = (ta == a) & (tg == g)

            @pl.when(mine)
            def _():
                pltpu.make_async_copy(src, dst, local).start()

            @pl.when(jnp.logical_not(mine))
            def _():
                pltpu.make_async_remote_copy(
                    src_ref=src, dst_ref=dst, send_sem=send, recv_sem=recv, device_id=(ta, tg), device_id_type=MESH
                ).start()

            return carry

        lax.fori_loop(0, CHUNK, send_step, 0)
        return carry

    lax.fori_loop(0, CHUNKS, x_step, 0)

    for copy in loads[2:]:
        copy.wait()
    pltpu.make_async_copy(slots.at[0], rec.at[0], local).wait()
    most = rec.at[pl.ds(0, DEV - 1)]
    pltpu.make_async_copy(most, most, recv).wait()

    special = (a == 0) & (g == 0)
    flag = jnp.where(special, 1.0, 0.0).astype(F32)

    def rec_of(row):
        return jnp.concatenate([rec[GY * t + row] for t in range(TA)], axis=0)

    def time_step(q, carry):
        z = []
        for n in range(4):
            pair = 4 * n + q
            left = rec_of(2 * pair)
            right = rec_of(2 * pair + 1)
            v = jnp.dot(tt[...], jnp.concatenate([left, right], axis=1), preferred_element_type=F32)
            ve, vo = halves(v[:, :128], v[:, 128:])
            re0 = ve[:32] + flag * ve[288:320]
            im0 = ve[128:160] - flag * ve[256:288]
            re = jnp.concatenate([re0, ve[32:128], vo[:128], ve[256:288]], axis=0)
            im = jnp.concatenate([im0, ve[160:256], vo[128:256], ve[288:320]], axis=0)
            z.append((re, im))
        (ar, ai), (br, bi), (cr, ci), (dr, di) = z
        sr, si, tr, ti = ar + cr, ai + ci, br + dr, bi + di
        er, ei, fr, fi = ar - cr, ai - ci, br - dr, bi - di
        lanes = pl.ds(pl.multiple_of(128 * q, 128), 128)
        for ref, re, im in (
            (u0, sr + tr, si + ti),
            (u1, er + fi, ei - fr),
            (u2, sr - tr, si - ti),
            (u3, er - fi, ei + fr),
        ):
            ref[:288, lanes] = re.astype(BF16)
            ref[288:, lanes] = im.astype(BF16)
        return carry

    lax.fori_loop(0, 4, time_step, 0)

    def products(ref, table):
        both = jnp.dot(ref[...], table, preferred_element_type=F32)
        return both[:288, :128], both[:288, 128:], both[288:, :128], both[288:, 128:]

    def plus(p1, p2, p3, p4):
        re, im = p1 + p4, p3 - p2
        return (re * re + im * im) * scale

    def minus(p1, p2, p3, p4):
        re, im = p1 - p4, p3 + p2
        return (re * re + im * im) * scale

    def y_step(a):
        def put(ref, block, quarter, value):
            lanes = pl.ds(pl.multiple_of(512 * block + 128 * quarter, 128), 128)
            ref[:, lanes] = value.astype(BF16)

        def mirrored(value):
            return jnp.concatenate([jnp.where(special, value[256:], value[:32]), value[32:256]], axis=0)

        for c, ref in ((0, u0), (2, u2)):
            parts = products(ref, ty[c // 2, a])
            put(power_d, a, c, plus(*parts)[:256])
            put(power_m, a, c, mirrored(minus(*parts)))
        up = plus(*products(u1, ty[2, a]))
        put(power_d, a, 1, up[:256])
        put(power_m, 3 - a, 3, mirrored(up))
        down = minus(*products(u3, ty[2, a]))
        put(power_m, a, 1, mirrored(down))
        put(power_d, 3 - a, 3, down[:256])

    h = g // HALF
    group = jnp.where(h == 0, g, GY - 1 - g)
    part = a + TA * h

    def send_block(member):
        ta, th = member % TA, member // TA
        tg = jnp.where(th == 0, group, GY - 1 - group)
        src = blocks.at[member]
        dst = out.at[jnp.where(th == 0, part, 7 - part)]

        @pl.when(member == part)
        def _():
            pltpu.make_async_copy(src, dst, local2).start()

        @pl.when(member != part)
        def _():
            pltpu.make_async_remote_copy(
                src_ref=src, dst_ref=dst, send_sem=send2, recv_sem=recv2, device_id=(ta, tg), device_id_type=MESH
            ).start()

    def row_step(a):
        lanes = pl.ds(pl.multiple_of(512 * a, 512), 512)
        both = jnp.dot(rows_m[...], power_m[:, lanes], preferred_element_type=F32).astype(BF16)
        blocks[4 + a] = both[:256]
        corner[a] = both[256:]
        send_block(4 + a)
        blocks[a] = jnp.dot(rows_d[...], power_d[:, lanes], preferred_element_type=F32).astype(BF16)
        send_block(a)

    def pair_step(i, carry):
        y_step(i)
        y_step(3 - i)
        row_step(i)
        row_step(3 - i)
        return carry

    lax.fori_loop(0, 2, pair_step, 0)
    has_corner = part == 0
    corner_to = GY - 1 - (group + HALF - 1) % HALF

    @pl.when(has_corner)
    def _():
        for ta in range(TA):
            pltpu.make_async_remote_copy(
                src_ref=corner.at[ta], dst_ref=corner_out, send_sem=corner_send, recv_sem=corner_recv,
                device_id=(ta, corner_to), device_id_type=MESH,
            ).start()
        pltpu.make_async_copy(corner, corner, corner_send).wait()

    @pl.when(h == 1)
    def _():
        pltpu.make_async_copy(corner_out, corner_out, corner_recv).wait()

    pltpu.make_async_copy(most, most, send).wait()
    pltpu.make_async_copy(blocks.at[0], out.at[0], local2).wait()
    seven = out.at[pl.ds(0, 7)]
    pltpu.make_async_copy(seven, seven, recv2).wait()
    pltpu.make_async_copy(seven, seven, send2).wait()


def fused(field, xt, tt, ty, rows_d, rows_m, scale):
    anywhere = pl.BlockSpec(memory_space=pl.ANY)
    operands = (field, xt, tt, ty, rows_d, rows_m)
    half = (FT * YL, NX // 2)
    dma = pltpu.SemaphoreType.DMA
    return pl.pallas_call(
        functools.partial(fused_kernel, scale),
        out_shape=(
            jax.ShapeDtypeStruct((8, 256, 512), BF16),
            jax.ShapeDtypeStruct((32, 512), BF16),
        ),
        in_specs=[anywhere] * 6,
        out_specs=(anywhere, anywhere),
        scratch_shapes=[pltpu.VMEM(x.shape, BF16) for x in operands]
        + [pltpu.VMEM(half, BF16)] * 2
        + [pltpu.VMEM((DEV, 8 * FT, 128), BF16)] * 2
        + [pltpu.VMEM((576, 512), BF16)] * 4
        + [pltpu.VMEM((256, 2048), BF16)] * 2
        + [pltpu.VMEM((8, 256, 512), BF16), pltpu.VMEM((4, 32, 512), BF16)]
        + [dma((6,))]
        + [dma] * 8,
        compiler_params=pltpu.CompilerParams(collective_id=3, has_side_effects=True, vmem_limit_bytes=56 * MIB),
        name="fused",
    )(*operands)


def last_kernel(block, below, corner, order, out):
    m = pl.program_id(0)
    mirrored = lax.axis_index("gy") >= HALF
    here = jnp.dot(block[0], order[...], preferred_element_type=F32).reshape(FR, 8, 512)
    out[...] = here

    @pl.when(mirrored)
    def _():
        low = jnp.dot(below[0], order[...], preferred_element_type=F32).reshape(FR, 8, 512)
        first = lax.broadcasted_iota(jnp.int32, (FR, 8, 512), 1) == 0
        out[...] = jnp.where(first, low, here)

        @pl.when(m == 0)
        def _():
            edge = jnp.dot(corner[...], order[...], preferred_element_type=F32)
            out[:, 0:1, :] = edge.reshape(FR, 1, 512)


def last_step(blocks, corner, order):
    return pl.pallas_call(
        last_kernel,
        grid=(8,),
        out_shape=jax.ShapeDtypeStruct((FR, 64, 512), F32),
        in_specs=[
            pl.BlockSpec((1, 256, 512), lambda m: (m, 0, 0)),
            pl.BlockSpec((1, 256, 512), lambda m: (jnp.maximum(m - 1, 0), 0, 0)),
            pl.BlockSpec((32, 512), lambda m: (0, 0)),
            pl.BlockSpec((512, 512), lambda m: (0, 0)),
        ],
        out_specs=pl.BlockSpec((FR, 8, 512), lambda m: (0, m, 0)),
        compiler_params=pltpu.CompilerParams(vmem_limit_bytes=32 * MIB),
        name="last_step",
    )(blocks, blocks, corner, order)


def shards(charge_field):
    tt, wsum = t_table()
    tables = [jnp.asarray(x) for x in (x_tables(), tt, y_tables(), *row_tables())]
    blocks, corner = fused(charge_field, *tables, 1.0 / (NX * NY * wsum))
    return last_step(blocks, corner, jnp.asarray(ky_table()))


def solution(mesh):
    return jax.shard_map(
        shards, mesh=mesh, in_specs=(P("ta", "gy", None),), out_specs=P(None, "gy", "ta"), check_vma=False
    )
```

```python
import functools
import math

import jax
import jax.numpy as jnp
import ml_dtypes
import numpy as np
from jax import lax
from jax.experimental import pallas as pl
from jax.experimental.pallas import tpu as pltpu
from jax.sharding import PartitionSpec as P

FR, NX, NY = 32, 2048, 2048
TA, GY = 4, 32
DEV = TA * GY
FT = FR // TA
YL = NY // GY
SLOT = 8
HALF = GY // 2
F32, BF16 = jnp.float32, jnp.bfloat16
MIB = 1 << 20


def bf(a):
    return np.asarray(a).astype(np.float32).astype(ml_dtypes.bfloat16)


def place(group, part):
    a, h = part % TA, part // TA
    return a, group if h == 0 else GY - 1 - group


def order_of(a, g):
    y, core = 2 * (a // 2) + g // 16, a % 2
    z, x = g // 4 % 4, g % 4
    return ((x + y + z) % 4 * 2 + core) * 16 + 4 * y + x


@functools.lru_cache(None)
def x_tables():
    kx = np.zeros((2, DEV, 4), np.int64)
    for group in range(HALF):
        for part in range(8):
            for parity in range(2):
                base = 64 * group + 8 * part + parity
                kx[parity, order_of(*place(group, part))] = base + 2 * np.arange(4)
    n = np.arange(NX // 2)
    angle = 2 * np.pi * ((kx[..., None] * n) % NX) / NX
    re, im = np.cos(angle), -np.sin(angle)
    zero = order_of(*place(0, 0))
    im[0, zero, 0] = np.cos(np.pi * n)
    both = np.stack([re, im], axis=2)
    return bf(both.reshape(2, DEV * 8, NX // 2))


@functools.lru_cache(None)
def t_table():
    t = np.arange(FR)
    window = 0.5 - 0.5 * np.cos(2 * np.pi * (t + 0.5) / FR)
    angle = 2 * np.pi * ((t[:, None] * t[None, :]) % FR) / FR
    cw, sw = np.cos(angle) * window, np.sin(angle) * window
    out = np.zeros((2, 4, FR, FR, 2, 4))
    for p in range(4):
        out[0, p, :, :, 0, p] = cw
        out[0, p, :, :, 1, p] = sw
        out[1, p, :, :, 0, p] = -sw
        out[1, p, :, :, 1, p] = cw
    extra = np.zeros((2, FR, FR, 2, 4))
    extra[0, :, :, 1, 0] = cw
    extra[1, :, :, 1, 0] = -sw
    k = FR * 8
    return bf(np.concatenate([out.reshape(k, k), extra.reshape(2 * FR, k)])), float(np.sum(window * window))


@functools.lru_cache(None)
def y_tables():
    n, k = np.arange(NY // 4), np.arange(NY // 4)
    out = []
    for q in (0, 2, 1):
        angle = 2 * np.pi * ((n[:, None] * (4 * k[None, :] + q)) % NY) / NY
        cs = np.stack([np.cos(angle).reshape(-1, 4, 128), np.sin(angle).reshape(-1, 4, 128)], axis=2)
        out.append(cs.transpose(1, 0, 2, 3).reshape(4, NY // 4, 256))
    return bf(np.stack(out))


@functools.lru_cache(None)
def row_tables():
    direct = np.zeros((FR, 8, 2, 4, FR))
    mirror = np.zeros((FR, 8, 2, 4, FR))
    corner = np.zeros((FR, 2, 4, FR))
    for w in range(FR):
        for j in range(8):
            direct[w, j, j % 2, j // 2, w] = 1
            mirror[w, (8 - j) % 8, j % 2, j // 2, -w % FR] = 1
        corner[w, 0, 0, -w % FR] = 1
    k = FR * 8
    return bf(direct.reshape(k, k)), bf(np.concatenate([mirror.reshape(k, k), corner.reshape(FR, k)]))


@functools.lru_cache(None)
def ky_table():
    out = np.zeros((4, 128, 128, 4))
    k = np.arange(128)
    for q in range(3):
        out[q, k, k, q] = 1
    out[3, k, 127 - k, 3] = 1
    return bf(out.reshape(512, 512))


def halves(first, second):
    low = lax.broadcasted_iota(jnp.int32, first.shape, first.ndim - 1) < 64
    one = jnp.where(low, first, pltpu.roll(second, 64, first.ndim - 1))
    two = jnp.where(low, pltpu.roll(first, 64, first.ndim - 1), second)
    return one, two


NT = (((1,), (1,)), ((), ()))
MESH = pl.DeviceIdType.MESH
CHUNKS = 8
CHUNK = DEV // CHUNKS
PIECE = 64


def fused_kernel(
    scale, field_in, xt_in, tt_in, ty_in, rd_in, rm_in, out, corner_out,
    field, xt, tt, ty, rows_d, rows_m, even, odd, slots, rec, u0, u1, u2, u3, power_d, power_m, blocks, corner,
    frame_load, table_load, load, send, recv, local, send2, recv2, local2, corner_send, corner_recv,
):
    a, g = lax.axis_index("ta"), lax.axis_index("gy")
    me = a * GY + g
    my_y, my_core, my_z, my_x = 2 * (a // 2) + g // 16, a % 2, g // 4 % 4, g % 4

    first = (my_x + my_y + my_z) % 4 * 2 + my_core
    barrier = pltpu.get_barrier_semaphore()

    def frame(t):
        return pltpu.make_async_copy(field_in.at[t], field.at[t], frame_load.at[t])

    def table(c):
        rows = pl.ds(pl.multiple_of(128 * ((first + c) % CHUNKS), 128), 128)
        return pltpu.make_async_copy(xt_in.at[:, rows], xt.at[:, rows], table_load.at[c])

    loads = [
        pltpu.make_async_copy(src, dst, load.at[i])
        for i, (src, dst) in enumerate(((tt_in, tt), (ty_in, ty), (rd_in, rows_d), (rm_in, rows_m)))
    ]

    def start_frame(t, carry):
        frame(t).start()
        return carry

    lax.fori_loop(0, FT, start_frame, 0)
    table(0).start()

    def greet(o, carry):
        peer = (me + o) % DEV
        pl.semaphore_signal(barrier, inc=1, device_id=(peer // GY, peer % GY), device_id_type=MESH)
        return carry

    lax.fori_loop(1, DEV, greet, 0)

    def start_table(c, carry):
        table(c).start()
        return carry

    lax.fori_loop(1, CHUNKS, start_table, 0)

    def fold(t, carry):
        frame(t).wait()
        rows = pl.ds(pl.multiple_of(YL * t, YL), YL)
        lo = field[t, :, : NX // 2].astype(F32)
        hi = field[t, :, NX // 2 :].astype(F32)
        even[rows] = (lo + hi).astype(BF16)
        odd[rows] = (lo - hi).astype(BF16)
        return carry

    lax.fori_loop(0, FT, fold, 0)
    for copy in loads:
        copy.start()

    def x_step(c, carry):
        table(c).wait()
        k = (first + c) % CHUNKS
        rows = pl.ds(pl.multiple_of(128 * k, 128), 128)
        for s in range(2):
            e = lax.dot_general(xt[0, rows], even[256 * s : 256 * (s + 1)], NT, preferred_element_type=F32)
            o = lax.dot_general(xt[1, rows], odd[256 * s : 256 * (s + 1)], NT, preferred_element_type=F32)
            for q in range(2):
                lanes = slice(128 * q, 128 * (q + 1))
                one, two = halves(e[:, lanes], o[:, lanes])
                both = jnp.concatenate([one.reshape(16, 8, 128), two.reshape(16, 8, 128)], axis=1)
                at = 16 * (2 * s + q)
                slots[pl.ds(16 * k, 16), at : at + 16] = both.astype(BF16)

        @pl.when(c == 0)
        def _():
            pl.semaphore_wait(barrier, DEV - 1)

        total, core = k // 2, k % 2

        def send_step(i, carry):
            y, x = (my_y + i // 4) % 4, (my_x + i % 4) % 4
            z = (total + 8 - x - y) % 4
            ta, tg = 2 * (y // 2) + core, 16 * (y % 2) + 4 * z + x
            src = slots.at[16 * k + 4 * y + x]
            dst = rec.at[me]
            mine = (ta == a) & (tg == g)

            @pl.when(mine)
            def _():
                pltpu.make_async_copy(src, dst, local).start()

            @pl.when(jnp.logical_not(mine))
            def _():
                pltpu.make_async_remote_copy(
                    src_ref=src, dst_ref=dst, send_sem=send, recv_sem=recv, device_id=(ta, tg), device_id_type=MESH
                ).start()

            return carry

        lax.fori_loop(0, CHUNK, send_step, 0)
        return carry

    lax.fori_loop(0, CHUNKS, x_step, 0)

    for copy in loads:
        copy.wait()
    pltpu.make_async_copy(slots.at[0], rec.at[0], local).wait()
    most = rec.at[pl.ds(0, DEV - 1)]
    pltpu.make_async_copy(most, most, recv).wait()

    special = (a == 0) & (g == 0)
    flag = jnp.where(special, 1.0, 0.0).astype(F32)

    def rec_of(row):
        return jnp.concatenate([rec[GY * t + row] for t in range(TA)], axis=0)

    def time_step(q, carry):
        z = []
        for n in range(4):
            pair = 4 * n + q
            left = rec_of(2 * pair)
            right = rec_of(2 * pair + 1)
            v = jnp.dot(tt[...], jnp.concatenate([left, right], axis=1), preferred_element_type=F32)
            ve, vo = halves(v[:, :128], v[:, 128:])
            re0 = ve[:32] + flag * ve[288:320]
            im0 = ve[128:160] - flag * ve[256:288]
            re = jnp.concatenate([re0, ve[32:128], vo[:128], ve[256:288]], axis=0)
            im = jnp.concatenate([im0, ve[160:256], vo[128:256], ve[288:320]], axis=0)
            z.append((re, im))
        (ar, ai), (br, bi), (cr, ci), (dr, di) = z
        sr, si, tr, ti = ar + cr, ai + ci, br + dr, bi + di
        er, ei, fr, fi = ar - cr, ai - ci, br - dr, bi - di
        lanes = pl.ds(pl.multiple_of(128 * q, 128), 128)
        for ref, re, im in (
            (u0, sr + tr, si + ti),
            (u1, er + fi, ei - fr),
            (u2, sr - tr, si - ti),
            (u3, er - fi, ei + fr),
        ):
            ref[:288, lanes] = re.astype(BF16)
            ref[288:, lanes] = im.astype(BF16)
        return carry

    lax.fori_loop(0, 4, time_step, 0)

    def products(ref, table):
        both = jnp.dot(ref[...], table, preferred_element_type=F32)
        return both[:288, :128], both[:288, 128:], both[288:, :128], both[288:, 128:]

    def plus(p1, p2, p3, p4):
        re, im = p1 + p4, p3 - p2
        return (re * re + im * im) * scale

    def minus(p1, p2, p3, p4):
        re, im = p1 - p4, p3 + p2
        return (re * re + im * im) * scale

    def put(ref, block, quarter, value):
        lanes = pl.ds(pl.multiple_of(512 * block + 128 * quarter, 128), 128)
        ref[:, lanes] = value.astype(BF16)

    def mirrored(value):
        return jnp.concatenate([jnp.where(special, value[256:], value[:32]), value[32:256]], axis=0)

    def odd_step(a):
        up = plus(*products(u1, ty[2, a]))
        put(power_d, a, 1, up[:256])
        put(power_m, 3 - a, 3, mirrored(up))
        down = minus(*products(u3, ty[2, a]))
        put(power_m, a, 1, mirrored(down))
        put(power_d, 3 - a, 3, down[:256])

    def even_step(a):
        for c, ref in ((0, u0), (2, u2)):
            parts = products(ref, ty[c // 2, a])
            put(power_d, a, c, plus(*parts)[:256])
            put(power_m, a, c, mirrored(minus(*parts)))

    h = g // HALF
    group = jnp.where(h == 0, g, GY - 1 - g)
    part = a + TA * h

    def send_piece(member, piece):
        ta, th = member % TA, member // TA
        tg = jnp.where(th == 0, group, GY - 1 - group)
        rows = pl.ds(pl.multiple_of(PIECE * piece, PIECE), PIECE)
        src = blocks.at[member, rows]
        dst = out.at[jnp.where(th == 0, part, 7 - part), rows]

        @pl.when(member == part)
        def _():
            pltpu.make_async_copy(src, dst, local2).start()

        @pl.when(member != part)
        def _():
            pltpu.make_async_remote_copy(
                src_ref=src, dst_ref=dst, send_sem=send2, recv_sem=recv2, device_id=(ta, tg), device_id_type=MESH
            ).start()

    def row_step(a):
        lanes = pl.ds(pl.multiple_of(512 * a, 512), 512)
        both = jnp.dot(rows_m[...], power_m[:, lanes], preferred_element_type=F32).astype(BF16)
        blocks[4 + a] = both[:256]
        corner[a] = both[256:]
        blocks[a] = jnp.dot(rows_d[...], power_d[:, lanes], preferred_element_type=F32).astype(BF16)

    def pair_step(i, carry):
        low = (i + my_core) % 2
        far = jnp.where(a // 2 == 0, 3 - low, low)
        odd_step(far)
        odd_step(3 - far)
        for to in (far, 3 - far):
            even_step(to)
            row_step(to)

        def pieces(n, carry):
            to = jnp.where(n % 4 < 2, far, 3 - far)
            send_piece(to + TA * ((n + 1) % 2), n // 4)
            return carry

        lax.fori_loop(0, 4 * (256 // PIECE), pieces, 0)
        return carry

    lax.fori_loop(0, 2, pair_step, 0)
    has_corner = part == 0
    corner_to = GY - 1 - (group + HALF - 1) % HALF

    @pl.when(has_corner)
    def _():
        for ta in range(TA):
            pltpu.make_async_remote_copy(
                src_ref=corner.at[ta], dst_ref=corner_out, send_sem=corner_send, recv_sem=corner_recv,
                device_id=(ta, corner_to), device_id_type=MESH,
            ).start()
        pltpu.make_async_copy(corner, corner, corner_send).wait()

    @pl.when(h == 1)
    def _():
        pltpu.make_async_copy(corner_out, corner_out, corner_recv).wait()

    pltpu.make_async_copy(most, most, send).wait()
    pltpu.make_async_copy(blocks.at[0], out.at[0], local2).wait()
    seven = out.at[pl.ds(0, 7)]
    pltpu.make_async_copy(seven, seven, recv2).wait()
    pltpu.make_async_copy(seven, seven, send2).wait()


def fused(field, xt, tt, ty, rows_d, rows_m, scale):
    anywhere = pl.BlockSpec(memory_space=pl.ANY)
    operands = (field, xt, tt, ty, rows_d, rows_m)
    half = (FT * YL, NX // 2)
    dma = pltpu.SemaphoreType.DMA
    return pl.pallas_call(
        functools.partial(fused_kernel, scale),
        out_shape=(
            jax.ShapeDtypeStruct((8, 256, 512), BF16),
            jax.ShapeDtypeStruct((32, 512), BF16),
        ),
        in_specs=[anywhere] * 6,
        out_specs=(anywhere, anywhere),
        scratch_shapes=[pltpu.VMEM(x.shape, BF16) for x in operands]
        + [pltpu.VMEM(half, BF16)] * 2
        + [pltpu.VMEM((DEV, 8 * FT, 128), BF16)] * 2
        + [pltpu.VMEM((576, 512), BF16)] * 4
        + [pltpu.VMEM((256, 2048), BF16)] * 2
        + [pltpu.VMEM((8, 256, 512), BF16), pltpu.VMEM((4, 32, 512), BF16)]
        + [dma((FT,)), dma((CHUNKS,)), dma((4,))]
        + [dma] * 8,
        compiler_params=pltpu.CompilerParams(collective_id=3, has_side_effects=True, vmem_limit_bytes=56 * MIB),
        name="fused",
    )(*operands)


LAST_STEPS = 2
LAST = FR // LAST_STEPS


def last_kernel(blocks, corner, order, out):
    mirrored = lax.axis_index("gy") >= HALF
    first = (lax.broadcasted_iota(jnp.int32, (LAST, 8, 512), 1) == 0) & mirrored
    edge = jnp.dot(corner[...], order[...], preferred_element_type=F32)
    below = jnp.broadcast_to(edge.reshape(LAST, 1, 512), (LAST, 8, 512))
    for m in range(8):
        here = jnp.dot(blocks[m], order[...], preferred_element_type=F32).reshape(LAST, 8, 512)
        out[:, 8 * m : 8 * m + 8] = jnp.where(first, below, here)
        below = here


def last_step(blocks, corner, order):
    return pl.pallas_call(
        last_kernel,
        grid=(LAST_STEPS,),
        out_shape=jax.ShapeDtypeStruct((FR, 64, 512), F32),
        in_specs=[
            pl.BlockSpec((8, LAST * 8, 512), lambda m: (0, m, 0)),
            pl.BlockSpec((LAST, 512), lambda m: (m, 0)),
            pl.BlockSpec((512, 512), lambda m: (0, 0)),
        ],
        out_specs=pl.BlockSpec((LAST, 64, 512), lambda m: (m, 0, 0)),
        compiler_params=pltpu.CompilerParams(vmem_limit_bytes=62 * MIB),
        name="last_step",
    )(blocks, corner, order)


def shards(charge_field):
    tt, wsum = t_table()
    tables = [jnp.asarray(x) for x in (x_tables(), tt, y_tables(), *row_tables())]
    blocks, corner = fused(charge_field, *tables, 1.0 / (NX * NY * wsum))
    return last_step(blocks, corner, jnp.asarray(ky_table()))


def solution(mesh):
    return jax.shard_map(
        shards, mesh=mesh, in_specs=(P("ta", "gy", None),), out_specs=P(None, "gy", "ta"), check_vma=False
    )
```

```python
import functools
import math

import jax
import jax.numpy as jnp
import ml_dtypes
import numpy as np
from jax import lax
from jax.experimental import pallas as pl
from jax.experimental.pallas import tpu as pltpu
from jax.sharding import PartitionSpec as P

FR, NX, NY = 32, 2048, 2048
TA, GY = 4, 32
DEV = TA * GY
FT = FR // TA
YL = NY // GY
SLOT = 8
HALF = GY // 2
F32, BF16 = jnp.float32, jnp.bfloat16
MIB = 1 << 20


def bf(a):
    return np.asarray(a).astype(np.float32).astype(ml_dtypes.bfloat16)


def place(group, part):
    a, h = part % TA, part // TA
    return a, group if h == 0 else GY - 1 - group


def order_of(a, g):
    y, core = 2 * (a // 2) + g // 16, a % 2
    z, x = g // 4 % 4, g % 4
    return ((x + y + z) % 4 * 2 + core) * 16 + 4 * y + x


@functools.lru_cache(None)
def x_tables():
    kx = np.zeros((2, DEV, 4), np.int64)
    for group in range(HALF):
        for part in range(8):
            for parity in range(2):
                base = 64 * group + 8 * part + parity
                kx[parity, order_of(*place(group, part))] = base + 2 * np.arange(4)
    n = np.arange(NX // 2)
    angle = 2 * np.pi * ((kx[..., None] * n) % NX) / NX
    re, im = np.cos(angle), -np.sin(angle)
    zero = order_of(*place(0, 0))
    im[0, zero, 0] = np.cos(np.pi * n)
    both = np.stack([re, im], axis=2)
    return bf(both.reshape(2, DEV * 8, NX // 2))


@functools.lru_cache(None)
def t_table():
    t = np.arange(FR)
    window = 0.5 - 0.5 * np.cos(2 * np.pi * (t + 0.5) / FR)
    angle = 2 * np.pi * ((t[:, None] * t[None, :]) % FR) / FR
    out = np.zeros((2, 4, FR, FR, 4))
    for p in range(4):
        out[0, p, :, :, p] = np.cos(angle) * window
        out[1, p, :, :, p] = np.sin(angle) * window
    return bf(out.reshape(2 * 4 * FR, FR * 4)), float(np.sum(window * window))


@functools.lru_cache(None)
def y_tables():
    n, k = np.arange(NY // 4), np.arange(NY // 4)
    out = []
    for q in (0, 2, 1):
        angle = 2 * np.pi * ((n[:, None] * (4 * k[None, :] + q)) % NY) / NY
        cs = np.stack([np.cos(angle).reshape(-1, 4, 128), np.sin(angle).reshape(-1, 4, 128)], axis=2)
        out.append(cs.transpose(1, 0, 2, 3).reshape(4, NY // 4, 256))
    return bf(np.stack(out))


@functools.lru_cache(None)
def row_tables():
    out = np.zeros((2, FR, 8, 2, 4, FR))
    for w in range(FR):
        for j in range(8):
            out[0, w, j, j % 2, j // 2, w] = 1
            out[1, w, (8 - j) % 8, j % 2, j // 2, -w % FR] = 1
    return bf(out.reshape(2, FR * 8, FR * 8))


@functools.lru_cache(None)
def ky_table():
    out = np.zeros((4, 128, 128, 4))
    k = np.arange(128)
    for q in range(3):
        out[q, k, k, q] = 1
    out[3, k, 127 - k, 3] = 1
    return bf(out.reshape(512, 512))


def halves(first, second):
    low = lax.broadcasted_iota(jnp.int32, first.shape, first.ndim - 1) < 64
    one = jnp.where(low, first, pltpu.roll(second, 64, first.ndim - 1))
    two = jnp.where(low, pltpu.roll(first, 64, first.ndim - 1), second)
    return one, two


NT = (((1,), (1,)), ((), ()))
MESH = pl.DeviceIdType.MESH
CHUNKS = 8
CHUNK = DEV // CHUNKS
PIECES = 128, 64


def fused_kernel(
    scale, field_in, xt_in, tt_in, ty_in, out, corner_out,
    field, xt, tt, ty, folded, slots, rec, u0, u1, u2, u3, blocks,
    frame_load, table_load, load, send, recv, local, send2, recv2, local2, corner_send, corner_recv,
):
    a, g = lax.axis_index("ta"), lax.axis_index("gy")
    me = a * GY + g
    my_y, my_core, my_z, my_x = 2 * (a >> 1) + (g >> 4), a & 1, (g >> 2) & 3, g & 3
    first = ((my_x + my_y + my_z) & 3) * 2 + my_core
    barrier = pltpu.get_barrier_semaphore()

    def frame(t):
        return pltpu.make_async_copy(field_in.at[t], field.at[t], frame_load.at[t])

    def table(s, c):
        rows = pl.ds(pl.multiple_of(128 * ((first + c) & 7), 128), 128)
        return pltpu.make_async_copy(xt_in.at[s, rows], xt.at[s, rows], table_load.at[s, c])

    loads = [pltpu.make_async_copy(src, dst, load.at[i]) for i, (src, dst) in enumerate(((tt_in, tt), (ty_in, ty)))]

    for t in range(FT):
        frame(t).start()
    table(0, 0).start()

    for t in range(FT):
        for o in range(max(16 * t, 1), 16 * (t + 1)):
            peer = (me + o) & (DEV - 1)
            pl.semaphore_signal(barrier, inc=1, device_id=(peer >> 5, peer & 31), device_id_type=MESH)
        frame(t).wait()
        rows = slice(YL * t, YL * (t + 1))
        lo = field[t, :, : NX // 2].astype(F32)
        hi = field[t, :, NX // 2 :].astype(F32)
        folded[0, rows] = (lo + hi).astype(BF16)
        folded[1, rows] = (lo - hi).astype(BF16)

    for s in range(2):

        def start_table(c, carry):
            table(s, c).start()
            return carry

        lax.fori_loop(1 - s, CHUNKS, start_table, 0)
    for copy in loads:
        copy.start()

    def x_step(s, c):
        table(s, c).wait()
        k = (first + c) & 7
        rows = pl.ds(pl.multiple_of(128 * k, 128), 128)
        tile = (16, 8, 128)
        stay = (lax.broadcasted_iota(jnp.int32, tile, 1) < 4) == (lax.broadcasted_iota(jnp.int32, tile, 2) < 64)
        for n in range(2):
            both = lax.dot_general(
                xt[s, rows], folded[s, 256 * n : 256 * (n + 1)], NT, preferred_element_type=F32
            )
            parts = []
            for q in range(2):
                part = both[:, 128 * q : 128 * (q + 1)].reshape(tile)
                parts.append(jnp.where(stay, part, pltpu.roll(pltpu.roll(part, 64, 2), 4, 1)))
            slots[s, pl.ds(16 * k, 16), 16 * n : 16 * (n + 1)] = jnp.concatenate(parts, axis=1).astype(BF16)

        if s == 0:

            @pl.when(c == 0)
            def _():
                pl.semaphore_wait(barrier, DEV - 1)

        total, core = k >> 1, k & 1

        def send_step(i, carry):
            y, x = (my_y + (i >> 2)) & 3, (my_x + i) & 3
            z = (total + 8 - x - y) & 3
            ta, tg = 2 * (y >> 1) + core, 16 * (y & 1) + 4 * z + x
            src = slots.at[s, 16 * k + 4 * y + x]
            dst = rec.at[s, me]
            mine = (ta == a) & (tg == g)

            @pl.when(mine)
            def _():
                pltpu.make_async_copy(src, dst, local.at[s]).start()

            @pl.when(jnp.logical_not(mine))
            def _():
                pltpu.make_async_remote_copy(
                    src_ref=src, dst_ref=dst, send_sem=send, recv_sem=recv.at[s], device_id=(ta, tg), device_id_type=MESH
                ).start()

            return carry

        lax.fori_loop(0, CHUNK, send_step, 0)

    for s in range(2):

        def step(c, carry):
            x_step(s, c)
            return carry

        lax.fori_loop(0, CHUNKS, step, 0)

    for copy in loads:
        copy.wait()

    special = (a == 0) & (g == 0)
    keep = jnp.where(special, 0.0, 1.0).astype(F32)
    h = g >> 4
    group = jnp.where(h == 0, g, GY - 1 - g)
    part = a + TA * h

    def send_piece(s, member, piece, size):
        ta, th = member & 3, member >> 2
        tg = jnp.where(th == 0, group, GY - 1 - group)
        rows = pl.ds(pl.multiple_of(size * piece, size), size)
        to_rows = pl.ds(pl.multiple_of(128 * s + size * piece, size), size)
        src = blocks.at[s, member, rows]
        dst = out.at[jnp.where(th == 0, part, 7 - part), to_rows]

        @pl.when(member == part)
        def _():
            pltpu.make_async_copy(src, dst, local2).start()

        @pl.when(member != part)
        def _():
            pltpu.make_async_remote_copy(
                src_ref=src, dst_ref=dst, send_sem=send2, recv_sem=recv2, device_id=(ta, tg), device_id_type=MESH
            ).start()

    def plus(p1, p2, p3, p4):
        re, im = p1 + p4, p3 - p2
        return (re * re + im * im) * scale

    def minus(p1, p2, p3, p4):
        re, im = p1 - p4, p3 + p2
        return (re * re + im * im) * scale

    most = rec.at[0, pl.ds(0, DEV - 1)]
    corner_to = GY - 1 - ((group + HALF - 1) & (HALF - 1))

    for s in range(2):
        count = 160 if s == 0 else 128
        size = PIECES[s]
        pltpu.make_async_copy(slots.at[s, 0], rec.at[s, 0], local.at[s]).wait()
        pltpu.make_async_copy(most, most, recv.at[s]).wait()

        def rec_of(row):
            return jnp.concatenate([rec[s, GY * t + row] for t in range(TA)], axis=0)

        def time_step(q, carry):
            z = []
            for n in range(4):
                pair = 4 * n + q
                x = jnp.concatenate([rec_of(2 * pair), rec_of(2 * pair + 1)], axis=1)
                v = jnp.dot(tt[...], x, preferred_element_type=F32)
                cr, ci = halves(v[:128, :128], v[:128, 128:])
                sr, si = halves(v[128:, :128], v[128:, 128:])
                if s == 0:
                    re = jnp.concatenate([cr[:32] + keep * si[:32], cr[32:] + si[32:], ci[:32]], axis=0)
                    im = jnp.concatenate([keep * ci[:32] - sr[:32], ci[32:] - sr[32:], -si[:32]], axis=0)
                else:
                    re, im = cr + si, ci - sr
                z.append((re, im))
            (ar, ai), (br, bi), (cr, ci), (dr, di) = z
            sr, si, tr, ti = ar + cr, ai + ci, br + dr, bi + di
            er, ei, fr, fi = ar - cr, ai - ci, br - dr, bi - di
            lanes = pl.ds(pl.multiple_of(128 * q, 128), 128)
            for ref, re, im in (
                (u0, sr + tr, si + ti),
                (u1, er + fi, ei - fr),
                (u2, sr - tr, si - ti),
                (u3, er - fi, ei + fr),
            ):
                ref[:count, lanes] = re.astype(BF16)
                ref[count : 2 * count, lanes] = im.astype(BF16)
            return carry

        lax.fori_loop(0, 4, time_step, 0)

        def products(ref, table):
            both = jnp.dot(ref[: 2 * count], table, preferred_element_type=F32)
            return both[:count, :128], both[:count, 128:], both[count:, :128], both[count:, 128:]

        def put(member, quarter, value):
            blocks[s, member, :, 128 * quarter : 128 * (quarter + 1)] = value.astype(BF16)

        def mirrored(value):
            if s == 1:
                return value
            return jnp.concatenate([jnp.where(special, value[128:], value[:32]), value[32:128]], axis=0)

        def odd_step(b):
            up = plus(*products(u1, ty[2, b]))
            put(b, 1, up[:128])
            put(7 - b, 3, mirrored(up))
            down = minus(*products(u3, ty[2, b]))
            put(4 + b, 1, mirrored(down))
            put(3 - b, 3, down[:128])

        def even_step(b):
            for c, ref in ((0, u0), (2, u2)):
                parts = products(ref, ty[c // 2, b])
                put(b, c, plus(*parts)[:128])
                put(4 + b, c, mirrored(minus(*parts)))

        def pair_step(i, carry):
            low = (i + my_core) & 1
            far = jnp.where(a >> 1 == 0, 3 - low, low)
            for b in (far, 3 - far):
                odd_step(b)
                even_step(b)

            def pieces(n, carry):
                to = jnp.where(n & 3 < 2, far, 3 - far)
                send_piece(s, to + TA * ((n + 1) & 1), n >> 2, size)
                return carry

            lax.fori_loop(0, 4 * (128 // size), pieces, 0)
            return carry

        lax.fori_loop(0, 2, pair_step, 0)
        if s == 0:

            @pl.when(part == 0)
            def _():
                for ta in range(TA):
                    pltpu.make_async_remote_copy(
                        src_ref=blocks.at[0, 4 + ta, pl.ds(0, FR)], dst_ref=corner_out,
                        send_sem=corner_send, recv_sem=corner_recv, device_id=(ta, corner_to), device_id_type=MESH,
                    ).start()

    @pl.when(part == 0)
    def _():
        all_corners = blocks.at[0, 0]
        pltpu.make_async_copy(all_corners, all_corners, corner_send).wait()

    @pl.when(h == 1)
    def _():
        pltpu.make_async_copy(corner_out, corner_out, corner_recv).wait()

    for s in range(2):
        pltpu.make_async_copy(most, most, send).wait()
    pltpu.make_async_copy(out.at[0], out.at[0], local2).wait()
    seven = out.at[pl.ds(0, 7)]
    pltpu.make_async_copy(seven, seven, recv2).wait()
    pltpu.make_async_copy(seven, seven, send2).wait()


def fused(field, xt, tt, ty, scale):
    anywhere = pl.BlockSpec(memory_space=pl.ANY)
    operands = (field, xt, tt, ty)
    dma = pltpu.SemaphoreType.DMA
    return pl.pallas_call(
        functools.partial(fused_kernel, scale),
        out_shape=(
            jax.ShapeDtypeStruct((8, 256, 512), BF16),
            jax.ShapeDtypeStruct((FR, 512), BF16),
        ),
        in_specs=[anywhere] * 4,
        out_specs=(anywhere, anywhere),
        scratch_shapes=[pltpu.VMEM(x.shape, BF16) for x in operands]
        + [pltpu.VMEM((2, FT * YL, NX // 2), BF16)]
        + [pltpu.VMEM((2, DEV, 4 * FT, 128), BF16)] * 2
        + [pltpu.VMEM((320, 512), BF16)] * 4
        + [pltpu.VMEM((2, 8, 128, 512), BF16)]
        + [dma((FT,)), dma((2, CHUNKS)), dma((2,)), dma, dma((2,)), dma((2,))]
        + [dma] * 5,
        compiler_params=pltpu.CompilerParams(collective_id=3, has_side_effects=True, vmem_limit_bytes=56 * MIB),
        name="fused",
    )(*operands)


LAST_STEPS = 2
LAST = 8 // LAST_STEPS


def last_kernel(blocks, corner, rows, order, out, turned, below):
    mirrored = lax.axis_index("gy") >= HALF
    rows_here = rows[jnp.where(mirrored, 1, 0)]
    first = (lax.broadcasted_iota(jnp.int32, (8 * FR, 512), 0) % 8 == 0) & mirrored

    @pl.when(pl.program_id(0) == 0)
    def _():
        edge = jnp.concatenate([corner[...], jnp.zeros((7 * FR, 512), BF16)], axis=0)
        below[...] = jnp.dot(rows_here, edge, preferred_element_type=F32)

    for m in range(LAST):
        here = jnp.dot(rows_here, blocks[m], preferred_element_type=F32)
        turned[m] = jnp.where(first, below[...], here).astype(BF16)
        below[...] = here
    for n in range(2):
        lanes = slice(256 * n, 256 * (n + 1))
        all_rows = turned[...].reshape(LAST * 8 * FR, 512)
        done = jnp.dot(all_rows, order[:, lanes], preferred_element_type=F32).reshape(LAST, FR, 8, 256)
        for m in range(LAST):
            out[:, 8 * m : 8 * m + 8, lanes] = done[m]


def last_step(blocks, corner, rows, order):
    return pl.pallas_call(
        last_kernel,
        grid=(LAST_STEPS,),
        out_shape=jax.ShapeDtypeStruct((FR, 64, 512), F32),
        in_specs=[
            pl.BlockSpec((LAST, 256, 512), lambda m: (m, 0, 0)),
            pl.BlockSpec((FR, 512), lambda m: (0, 0)),
            pl.BlockSpec((2, 256, 256), lambda m: (0, 0, 0)),
            pl.BlockSpec((512, 512), lambda m: (0, 0)),
        ],
        out_specs=pl.BlockSpec((FR, 8 * LAST, 512), lambda m: (0, m, 0)),
        scratch_shapes=[pltpu.VMEM((LAST, 8 * FR, 512), BF16), pltpu.VMEM((8 * FR, 512), F32)],
        compiler_params=pltpu.CompilerParams(vmem_limit_bytes=62 * MIB),
        name="last_step",
    )(blocks, corner, rows, order)


def shards(charge_field):
    tt, wsum = t_table()
    tables = [jnp.asarray(x) for x in (x_tables(), tt, y_tables())]
    blocks, corner = fused(charge_field, *tables, 1.0 / (NX * NY * wsum))
    return last_step(blocks, corner, jnp.asarray(row_tables()), jnp.asarray(ky_table()))


def solution(mesh):
    return jax.shard_map(
        shards, mesh=mesh, in_specs=(P("ta", "gy", None),), out_specs=P(None, "gy", "ta"), check_vma=False
    )
```

```python
import functools
import math

import jax
import jax.numpy as jnp
import ml_dtypes
import numpy as np
from jax import lax
from jax.experimental import pallas as pl
from jax.experimental.pallas import tpu as pltpu
from jax.sharding import PartitionSpec as P

FR, NX, NY = 32, 2048, 2048
TA, GY = 4, 32
DEV = TA * GY
FT = FR // TA
YL = NY // GY
SLOT = 8
HALF = GY // 2
F32, BF16 = jnp.float32, jnp.bfloat16
MIB = 1 << 20


def bf(a):
    return np.asarray(a).astype(np.float32).astype(ml_dtypes.bfloat16)


def place(group, part):
    a, h = part % TA, part // TA
    return a, group if h == 0 else GY - 1 - group


def order_of(a, g):
    y, core = 2 * (a // 2) + g // 16, a % 2
    z, x = g // 4 % 4, g % 4
    return ((x + y + z) % 4 * 2 + core) * 16 + 4 * y + x


@functools.lru_cache(None)
def x_tables():
    kx = np.zeros((2, DEV, 4), np.int64)
    for group in range(HALF):
        for part in range(8):
            for parity in range(2):
                base = 64 * group + 8 * part + parity
                kx[parity, order_of(*place(group, part))] = base + 2 * np.arange(4)
    n = np.arange(NX // 2)
    angle = 2 * np.pi * ((kx[..., None] * n) % NX) / NX
    re, im = np.cos(angle), -np.sin(angle)
    zero = order_of(*place(0, 0))
    im[0, zero, 0] = np.cos(np.pi * n)
    both = np.stack([re, im], axis=2)
    return bf(both.reshape(2, DEV * 8, NX // 2))


@functools.lru_cache(None)
def t_table():
    t = np.arange(FR)
    window = 0.5 - 0.5 * np.cos(2 * np.pi * (t + 0.5) / FR)
    angle = 2 * np.pi * ((t[:, None] * t[None, :]) % FR) / FR
    out = np.zeros((2, 4, FR, FR, 4))
    for p in range(4):
        out[0, p, :, :, p] = np.cos(angle) * window
        out[1, p, :, :, p] = np.sin(angle) * window
    return bf(out.reshape(2 * 4 * FR, FR * 4)), float(np.sum(window * window))


@functools.lru_cache(None)
def y_tables():
    n, k = np.arange(NY // 4), np.arange(NY // 4)
    out = []
    for q in (0, 2, 1):
        angle = 2 * np.pi * ((n[:, None] * (4 * k[None, :] + q)) % NY) / NY
        cs = np.stack([np.cos(angle).reshape(-1, 4, 128), np.sin(angle).reshape(-1, 4, 128)], axis=2)
        out.append(cs.transpose(1, 0, 2, 3).reshape(4, NY // 4, 256))
    return bf(np.stack(out))


@functools.lru_cache(None)
def row_tables():
    out = np.zeros((2, FR, 8, 2, 4, FR))
    for w in range(FR):
        for j in range(8):
            out[0, w, j, j % 2, j // 2, w] = 1
            out[1, w, (8 - j) % 8, j % 2, j // 2, -w % FR] = 1
    return bf(out.reshape(2, FR * 8, FR * 8))


@functools.lru_cache(None)
def ky_table():
    out = np.zeros((4, 128, 128, 4))
    k = np.arange(128)
    for q in range(3):
        out[q, k, k, q] = 1
    out[3, k, 127 - k, 3] = 1
    return bf(out.reshape(512, 512))


def halves(first, second):
    low = lax.broadcasted_iota(jnp.int32, first.shape, first.ndim - 1) < 64
    one = jnp.where(low, first, pltpu.roll(second, 64, first.ndim - 1))
    two = jnp.where(low, pltpu.roll(first, 64, first.ndim - 1), second)
    return one, two


NT = (((1,), (1,)), ((), ()))
MESH = pl.DeviceIdType.MESH
CHUNKS = 8
CHUNK = DEV // CHUNKS
PIECES = 128, 64


def fused_kernel(
    scale, field_in, xt_in, tt_in, ty_in, out, corner_out,
    field, xt, tt, ty, folded, slots, rec, u0, u1, u2, u3, blocks,
    frame_load, table_load, load, send, recv, local, send2, recv2, local2, corner_send, corner_recv,
):
    a, g = lax.axis_index("ta"), lax.axis_index("gy")
    me = a * GY + g
    my_y, my_core, my_z, my_x = 2 * (a >> 1) + (g >> 4), a & 1, (g >> 2) & 3, g & 3
    first = ((my_x + my_y + my_z) & 3) * 2 + my_core
    barrier = pltpu.get_barrier_semaphore()

    def frame(t):
        return pltpu.make_async_copy(field_in.at[t], field.at[t], frame_load.at[t])

    def table(s, c):
        rows = pl.ds(pl.multiple_of(128 * ((first + c) & 7), 128), 128)
        return pltpu.make_async_copy(xt_in.at[s, rows], xt.at[s, rows], table_load.at[s, c])

    loads = [pltpu.make_async_copy(src, dst, load.at[i]) for i, (src, dst) in enumerate(((tt_in, tt), (ty_in, ty)))]

    for t in range(FT):
        frame(t).start()
    table(0, 0).start()
    table(0, 1).start()

    for o in range(1, DEV):
        peer = (me + o) & (DEV - 1)
        pl.semaphore_signal(barrier, inc=1, device_id=(peer >> 5, peer & 31), device_id_type=MESH)

    for t in range(FT):
        frame(t).wait()
        rows = slice(YL * t, YL * (t + 1))
        lo = field[t, :, : NX // 2].astype(F32)
        hi = field[t, :, NX // 2 :].astype(F32)
        folded[0, rows] = (lo + hi).astype(BF16)
        folded[1, rows] = (lo - hi).astype(BF16)

    def x_step(s, c):
        table(s, c).wait()
        k = (first + c) & 7
        rows = pl.ds(pl.multiple_of(128 * k, 128), 128)
        tile = (16, 8, 128)
        stay = (lax.broadcasted_iota(jnp.int32, tile, 1) < 4) == (lax.broadcasted_iota(jnp.int32, tile, 2) < 64)
        for n in range(2):
            both = lax.dot_general(
                xt[s, rows], folded[s, 256 * n : 256 * (n + 1)], NT, preferred_element_type=F32
            )
            parts = []
            for q in range(2):
                part = both[:, 128 * q : 128 * (q + 1)].reshape(tile)
                parts.append(jnp.where(stay, part, pltpu.roll(pltpu.roll(part, 64, 2), 4, 1)))
            slots[s, pl.ds(16 * k, 16), 16 * n : 16 * (n + 1)] = jnp.concatenate(parts, axis=1).astype(BF16)

    def send_step(s, c):
        k = (first + c) & 7
        total, core = k >> 1, k & 1
        for i in range(CHUNK):
            y, x = (my_y + (i >> 2)) & 3, (my_x + i) & 3
            z = (total + 8 - x - y) & 3
            src = slots.at[s, 16 * k + 4 * y + x]
            dst = rec.at[s, me]
            if i == 0 and isinstance(c, int) and c == 0:
                pltpu.make_async_copy(src, dst, local.at[s]).start()
                continue
            pltpu.make_async_remote_copy(
                src_ref=src, dst_ref=dst, send_sem=send, recv_sem=recv.at[s],
                device_id=(2 * (y >> 1) + core, 16 * (y & 1) + 4 * z + x), device_id_type=MESH,
            ).start()

    for s in range(2):
        x_step(s, 0)
        if s == 0:
            pl.semaphore_wait(barrier, DEV - 1)
        else:
            send_step(0, CHUNKS - 1)
        send_step(s, 0)
        if s == 0:
            for c in range(2, CHUNKS):
                table(0, c).start()
            for c in range(CHUNKS):
                table(1, c).start()
        x_step(s, 1)

        def step(c, carry):
            send_step(s, c - 1)
            x_step(s, c)
            return carry

        lax.fori_loop(2, CHUNKS, step, 0)
        if s == 0:
            for copy in loads:
                copy.start()
    send_step(1, CHUNKS - 1)

    for copy in loads:
        copy.wait()

    special = (a == 0) & (g == 0)
    keep = jnp.where(special, 0.0, 1.0).astype(F32)
    h = g >> 4
    group = jnp.where(h == 0, g, GY - 1 - g)
    part = a + TA * h

    def send_piece(s, member, piece, size):
        ta, th = member & 3, member >> 2
        tg = jnp.where(th == 0, group, GY - 1 - group)
        rows = pl.ds(pl.multiple_of(size * piece, size), size)
        to_rows = pl.ds(pl.multiple_of(128 * s + size * piece, size), size)
        src = blocks.at[s, member, rows]
        dst = out.at[jnp.where(th == 0, part, 7 - part), to_rows]

        @pl.when(member == part)
        def _():
            pltpu.make_async_copy(src, dst, local2).start()

        @pl.when(member != part)
        def _():
            pltpu.make_async_remote_copy(
                src_ref=src, dst_ref=dst, send_sem=send2, recv_sem=recv2, device_id=(ta, tg), device_id_type=MESH
            ).start()

    def plus(p1, p2, p3, p4):
        re, im = p1 + p4, p3 - p2
        return (re * re + im * im) * scale

    def minus(p1, p2, p3, p4):
        re, im = p1 - p4, p3 + p2
        return (re * re + im * im) * scale

    most = rec.at[0, pl.ds(0, DEV - 1)]
    corner_to = GY - 1 - ((group + HALF - 1) & (HALF - 1))

    for s in range(2):
        count = 160 if s == 0 else 128
        size = PIECES[s]
        pltpu.make_async_copy(slots.at[s, 0], rec.at[s, 0], local.at[s]).wait()
        pltpu.make_async_copy(most, most, recv.at[s]).wait()

        def rec_of(row):
            return jnp.concatenate([rec[s, GY * t + row] for t in range(TA)], axis=0)

        def time_step(q, carry):
            z = []
            for n in range(4):
                pair = 4 * n + q
                x = jnp.concatenate([rec_of(2 * pair), rec_of(2 * pair + 1)], axis=1)
                v = jnp.dot(tt[...], x, preferred_element_type=F32)
                cr, ci = halves(v[:128, :128], v[:128, 128:])
                sr, si = halves(v[128:, :128], v[128:, 128:])
                if s == 0:
                    re = jnp.concatenate([cr[:32] + keep * si[:32], cr[32:] + si[32:], ci[:32]], axis=0)
                    im = jnp.concatenate([keep * ci[:32] - sr[:32], ci[32:] - sr[32:], -si[:32]], axis=0)
                else:
                    re, im = cr + si, ci - sr
                z.append((re, im))
            (ar, ai), (br, bi), (cr, ci), (dr, di) = z
            sr, si, tr, ti = ar + cr, ai + ci, br + dr, bi + di
            er, ei, fr, fi = ar - cr, ai - ci, br - dr, bi - di
            lanes = pl.ds(pl.multiple_of(128 * q, 128), 128)
            for ref, re, im in (
                (u0, sr + tr, si + ti),
                (u1, er + fi, ei - fr),
                (u2, sr - tr, si - ti),
                (u3, er - fi, ei + fr),
            ):
                ref[:count, lanes] = re.astype(BF16)
                ref[count : 2 * count, lanes] = im.astype(BF16)
            return carry

        lax.fori_loop(0, 4, time_step, 0)

        def products(ref, table):
            both = jnp.dot(ref[: 2 * count], table, preferred_element_type=F32)
            return both[:count, :128], both[:count, 128:], both[count:, :128], both[count:, 128:]

        def put(member, quarter, value):
            blocks[s, member, :, 128 * quarter : 128 * (quarter + 1)] = value.astype(BF16)

        def mirrored(value):
            if s == 1:
                return value
            return jnp.concatenate([jnp.where(special, value[128:], value[:32]), value[32:128]], axis=0)

        def odd_step(b):
            up = plus(*products(u1, ty[2, b]))
            put(b, 1, up[:128])
            put(7 - b, 3, mirrored(up))
            down = minus(*products(u3, ty[2, b]))
            put(4 + b, 1, mirrored(down))
            put(3 - b, 3, down[:128])

        def even_step(b):
            for c, ref in ((0, u0), (2, u2)):
                parts = products(ref, ty[c // 2, b])
                put(b, c, plus(*parts)[:128])
                put(4 + b, c, mirrored(minus(*parts)))

        def pair_step(i, carry):
            low = (i + my_core) & 1
            far = jnp.where(a >> 1 == 0, 3 - low, low)
            for b in (far, 3 - far):
                odd_step(b)
                even_step(b)

            def pieces(n, carry):
                to = jnp.where(n & 3 < 2, 3 - far, far)
                send_piece(s, to + TA * ((n + 1) & 1), n >> 2, size)
                return carry

            lax.fori_loop(0, 4 * (128 // size), pieces, 0)
            return carry

        lax.fori_loop(0, 2, pair_step, 0)
        if s == 0:

            @pl.when(part == 0)
            def _():
                for ta in range(TA):
                    pltpu.make_async_remote_copy(
                        src_ref=blocks.at[0, 4 + ta, pl.ds(0, FR)], dst_ref=corner_out,
                        send_sem=corner_send, recv_sem=corner_recv, device_id=(ta, corner_to), device_id_type=MESH,
                    ).start()

    @pl.when(part == 0)
    def _():
        all_corners = blocks.at[0, 0]
        pltpu.make_async_copy(all_corners, all_corners, corner_send).wait()

    @pl.when(h == 1)
    def _():
        pltpu.make_async_copy(corner_out, corner_out, corner_recv).wait()

    for s in range(2):
        pltpu.make_async_copy(most, most, send).wait()
    pltpu.make_async_copy(out.at[0], out.at[0], local2).wait()
    seven = out.at[pl.ds(0, 7)]
    pltpu.make_async_copy(seven, seven, recv2).wait()
    pltpu.make_async_copy(seven, seven, send2).wait()


def fused(field, xt, tt, ty, scale):
    anywhere = pl.BlockSpec(memory_space=pl.ANY)
    operands = (field, xt, tt, ty)
    dma = pltpu.SemaphoreType.DMA
    return pl.pallas_call(
        functools.partial(fused_kernel, scale),
        out_shape=(
            jax.ShapeDtypeStruct((8, 256, 512), BF16),
            jax.ShapeDtypeStruct((FR, 512), BF16),
        ),
        in_specs=[anywhere] * 4,
        out_specs=(anywhere, anywhere),
        scratch_shapes=[pltpu.VMEM(x.shape, BF16) for x in operands]
        + [pltpu.VMEM((2, FT * YL, NX // 2), BF16)]
        + [pltpu.VMEM((2, DEV, 4 * FT, 128), BF16)] * 2
        + [pltpu.VMEM((320, 512), BF16)] * 4
        + [pltpu.VMEM((2, 8, 128, 512), BF16)]
        + [dma((FT,)), dma((2, CHUNKS)), dma((2,)), dma, dma((2,)), dma((2,))]
        + [dma] * 5,
        compiler_params=pltpu.CompilerParams(collective_id=3, has_side_effects=True, vmem_limit_bytes=56 * MIB),
        name="fused",
    )(*operands)


LAST_STEPS = 2
LAST = 8 // LAST_STEPS


def last_kernel(blocks, corner, rows, order, out, turned, below):
    mirrored = lax.axis_index("gy") >= HALF
    rows_here = rows[jnp.where(mirrored, 1, 0)]
    first = (lax.broadcasted_iota(jnp.int32, (8 * FR, 512), 0) % 8 == 0) & mirrored

    @pl.when(pl.program_id(0) == 0)
    def _():
        edge = jnp.concatenate([corner[...], jnp.zeros((7 * FR, 512), BF16)], axis=0)
        below[...] = jnp.dot(rows_here, edge, preferred_element_type=F32)

    for m in range(LAST):
        here = jnp.dot(rows_here, blocks[m], preferred_element_type=F32)
        turned[m] = jnp.where(first, below[...], here).astype(BF16)
        below[...] = here
    for n in range(2):
        lanes = slice(256 * n, 256 * (n + 1))
        all_rows = turned[...].reshape(LAST * 8 * FR, 512)
        done = jnp.dot(all_rows, order[:, lanes], preferred_element_type=F32).reshape(LAST, FR, 8, 256)
        for m in range(LAST):
            out[:, 8 * m : 8 * m + 8, lanes] = done[m]


def last_step(blocks, corner, rows, order):
    return pl.pallas_call(
        last_kernel,
        grid=(LAST_STEPS,),
        out_shape=jax.ShapeDtypeStruct((FR, 64, 512), F32),
        in_specs=[
            pl.BlockSpec((LAST, 256, 512), lambda m: (m, 0, 0)),
            pl.BlockSpec((FR, 512), lambda m: (0, 0)),
            pl.BlockSpec((2, 256, 256), lambda m: (0, 0, 0)),
            pl.BlockSpec((512, 512), lambda m: (0, 0)),
        ],
        out_specs=pl.BlockSpec((FR, 8 * LAST, 512), lambda m: (0, m, 0)),
        scratch_shapes=[pltpu.VMEM((LAST, 8 * FR, 512), BF16), pltpu.VMEM((8 * FR, 512), F32)],
        compiler_params=pltpu.CompilerParams(vmem_limit_bytes=62 * MIB),
        name="last_step",
    )(blocks, corner, rows, order)


def shards(charge_field):
    tt, wsum = t_table()
    tables = [jnp.asarray(x) for x in (x_tables(), tt, y_tables())]
    blocks, corner = fused(charge_field, *tables, 1.0 / (NX * NY * wsum))
    return last_step(blocks, corner, jnp.asarray(row_tables()), jnp.asarray(ky_table()))


def solution(mesh):
    return jax.shard_map(
        shards, mesh=mesh, in_specs=(P("ta", "gy", None),), out_specs=P(None, "gy", "ta"), check_vma=False
    )
```

```python
import functools
import math

import jax
import jax.numpy as jnp
import ml_dtypes
import numpy as np
from jax import lax
from jax.experimental import pallas as pl
from jax.experimental.pallas import tpu as pltpu
from jax.sharding import PartitionSpec as P

FR, NX, NY = 32, 2048, 2048
TA, GY = 4, 32
DEV = TA * GY
FT = FR // TA
YL = NY // GY
SLOT = 8
HALF = GY // 2
F32, BF16 = jnp.float32, jnp.bfloat16
MIB = 1 << 20


def bf(a):
    return np.asarray(a).astype(np.float32).astype(ml_dtypes.bfloat16)


def place(group, part):
    a, h = part % TA, part // TA
    return a, group if h == 0 else GY - 1 - group


def order_of(a, g):
    y, core = 2 * (a // 2) + g // 16, a % 2
    z, x = g // 4 % 4, g % 4
    return ((x + y + z) % 4 * 2 + core) * 16 + 4 * y + x


@functools.lru_cache(None)
def x_tables():
    kx = np.zeros((2, DEV, 4), np.int64)
    for group in range(HALF):
        for part in range(8):
            for parity in range(2):
                base = 64 * group + 8 * part + parity
                kx[parity, order_of(*place(group, part))] = base + 2 * np.arange(4)
    n = np.arange(NX // 2)
    angle = 2 * np.pi * ((kx[..., None] * n) % NX) / NX
    re, im = np.cos(angle), -np.sin(angle)
    zero = order_of(*place(0, 0))
    im[0, zero, 0] = np.cos(np.pi * n)
    both = np.stack([re, im], axis=2)
    return bf(both.reshape(2, DEV * 8, NX // 2))


@functools.lru_cache(None)
def t_table():
    t = np.arange(FR)
    window = 0.5 - 0.5 * np.cos(2 * np.pi * (t + 0.5) / FR)
    angle = 2 * np.pi * ((t[:, None] * t[None, :]) % FR) / FR
    out = np.zeros((2, 4, FR, FR, 4))
    for p in range(4):
        out[0, p, :, :, p] = np.cos(angle) * window
        out[1, p, :, :, p] = np.sin(angle) * window
    return bf(out.reshape(2 * 4 * FR, FR * 4)), float(np.sum(window * window))


@functools.lru_cache(None)
def y_tables():
    n, k = np.arange(NY // 4), np.arange(NY // 4)
    out = []
    for q in (0, 2, 1):
        angle = 2 * np.pi * ((n[:, None] * (4 * k[None, :] + q)) % NY) / NY
        cs = np.stack([np.cos(angle).reshape(-1, 4, 128), np.sin(angle).reshape(-1, 4, 128)], axis=2)
        out.append(cs.transpose(1, 0, 2, 3).reshape(4, NY // 4, 256))
    return bf(np.stack(out))


@functools.lru_cache(None)
def row_tables():
    out = np.zeros((2, FR, 8, 2, 4, FR))
    for w in range(FR):
        for j in range(8):
            out[0, w, j, j % 2, j // 2, w] = 1
            out[1, w, (8 - j) % 8, j % 2, j // 2, -w % FR] = 1
    return bf(out.reshape(2, FR * 8, FR * 8))


@functools.lru_cache(None)
def ky_table():
    out = np.zeros((4, 128, 128, 4))
    k = np.arange(128)
    for q in range(3):
        out[q, k, k, q] = 1
    out[3, k, 127 - k, 3] = 1
    return bf(out.reshape(512, 512))


def halves(first, second):
    low = lax.broadcasted_iota(jnp.int32, first.shape, first.ndim - 1) < 64
    one = jnp.where(low, first, pltpu.roll(second, 64, first.ndim - 1))
    two = jnp.where(low, pltpu.roll(first, 64, first.ndim - 1), second)
    return one, two


NT = (((1,), (1,)), ((), ()))
MESH = pl.DeviceIdType.MESH
CHUNKS = 8
CHUNK = DEV // CHUNKS
PIECE = 32


def fused_kernel(
    scale, field_in, xt_in, tt_in, ty_in, out, corner_out,
    field, xt, tt, ty, folded, slots, rec, u0, u1, u2, u3, blocks,
    frame_load, table_load, load, send, recv, local, send2, recv2, local2, corner_send, corner_recv,
):
    a, g = lax.axis_index("ta"), lax.axis_index("gy")
    me = a * GY + g
    my_y, my_core, my_z, my_x = 2 * (a >> 1) + (g >> 4), a & 1, (g >> 2) & 3, g & 3
    first = ((my_x + my_y + my_z) & 3) * 2 + my_core
    barrier = pltpu.get_barrier_semaphore()

    def frame(t):
        return pltpu.make_async_copy(field_in.at[t], field.at[t], frame_load.at[t])

    def table(s, c):
        rows = pl.ds(pl.multiple_of(128 * ((first + c) & 7), 128), 128)
        return pltpu.make_async_copy(xt_in.at[s, rows], xt.at[s, rows], table_load.at[s, c])

    loads = [pltpu.make_async_copy(src, dst, load.at[i]) for i, (src, dst) in enumerate(((tt_in, tt), (ty_in, ty)))]

    for t in range(FT):
        frame(t).start()
    table(0, 0).start()
    table(0, 1).start()

    for o in range(1, DEV):
        peer = (me + o) & (DEV - 1)
        pl.semaphore_signal(barrier, inc=1, device_id=(peer >> 5, peer & 31), device_id_type=MESH)

    for t in range(FT):
        frame(t).wait()
        rows = slice(YL * t, YL * (t + 1))
        lo = field[t, :, : NX // 2].astype(F32)
        hi = field[t, :, NX // 2 :].astype(F32)
        folded[0, rows] = (lo + hi).astype(BF16)
        folded[1, rows] = (lo - hi).astype(BF16)

    def x_step(s, c):
        table(s, c).wait()
        k = (first + c) & 7
        rows = pl.ds(pl.multiple_of(128 * k, 128), 128)
        tile = (16, 8, 128)
        stay = (lax.broadcasted_iota(jnp.int32, tile, 1) < 4) == (lax.broadcasted_iota(jnp.int32, tile, 2) < 64)
        for n in range(2):
            both = lax.dot_general(
                xt[s, rows], folded[s, 256 * n : 256 * (n + 1)], NT, preferred_element_type=F32
            )
            parts = []
            for q in range(2):
                part = both[:, 128 * q : 128 * (q + 1)].reshape(tile)
                parts.append(jnp.where(stay, part, pltpu.roll(pltpu.roll(part, 64, 2), 4, 1)))
            slots[s, pl.ds(16 * k, 16), 16 * n : 16 * (n + 1)] = jnp.concatenate(parts, axis=1).astype(BF16)

    def send_step(s, c):
        k = (first + c) & 7
        total, core = k >> 1, k & 1
        for i in range(CHUNK):
            y, x = (my_y + (i >> 2)) & 3, (my_x + i) & 3
            z = (total + 8 - x - y) & 3
            src = slots.at[s, 16 * k + 4 * y + x]
            dst = rec.at[s, me]
            if i == 0 and isinstance(c, int) and c == 0:
                pltpu.make_async_copy(src, dst, local.at[s]).start()
                continue
            pltpu.make_async_remote_copy(
                src_ref=src, dst_ref=dst, send_sem=send, recv_sem=recv.at[s],
                device_id=(2 * (y >> 1) + core, 16 * (y & 1) + 4 * z + x), device_id_type=MESH,
            ).start()

    for s in range(2):
        x_step(s, 0)
        if s == 0:
            pl.semaphore_wait(barrier, DEV - 1)
        else:
            send_step(0, CHUNKS - 1)
        send_step(s, 0)
        if s == 0:
            for c in range(2, CHUNKS):
                table(0, c).start()
            for c in range(CHUNKS):
                table(1, c).start()
        x_step(s, 1)

        def step(c, carry):
            send_step(s, c - 1)
            x_step(s, c)
            return carry

        lax.fori_loop(2, CHUNKS, step, 0)
        if s == 0:
            for copy in loads:
                copy.start()
    send_step(1, CHUNKS - 1)

    for copy in loads:
        copy.wait()

    special = (a == 0) & (g == 0)
    keep = jnp.where(special, 0.0, 1.0).astype(F32)
    h = g >> 4
    group = jnp.where(h == 0, g, GY - 1 - g)
    part = a + TA * h

    def send_piece(s, member, piece):
        ta, th = member & 3, member >> 2
        tg = jnp.where(th == 0, group, GY - 1 - group)
        rows = pl.ds(pl.multiple_of(PIECE * piece, PIECE), PIECE)
        to_rows = pl.ds(pl.multiple_of(128 * s + PIECE * piece, PIECE), PIECE)
        src = blocks.at[s, member, rows]
        dst = out.at[jnp.where(th == 0, part, 7 - part), to_rows]

        @pl.when(member == part)
        def _():
            pltpu.make_async_copy(src, dst, local2).start()

        @pl.when(member != part)
        def _():
            pltpu.make_async_remote_copy(
                src_ref=src, dst_ref=dst, send_sem=send2, recv_sem=recv2, device_id=(ta, tg), device_id_type=MESH
            ).start()

    def plus(p1, p2, p3, p4):
        re, im = p1 + p4, p3 - p2
        return (re * re + im * im) * scale

    def minus(p1, p2, p3, p4):
        re, im = p1 - p4, p3 + p2
        return (re * re + im * im) * scale

    most = rec.at[0, pl.ds(0, DEV - 1)]
    corner_to = GY - 1 - ((group + HALF - 1) & (HALF - 1))

    for s in range(2):
        count = 160 if s == 0 else 128
        pltpu.make_async_copy(slots.at[s, 0], rec.at[s, 0], local.at[s]).wait()
        pltpu.make_async_copy(most, most, recv.at[s]).wait()

        def rec_of(row):
            return jnp.concatenate([rec[s, GY * t + row] for t in range(TA)], axis=0)

        def time_step(q, carry):
            z = []
            for n in range(4):
                pair = 4 * n + q
                x = jnp.concatenate([rec_of(2 * pair), rec_of(2 * pair + 1)], axis=1)
                v = jnp.dot(tt[...], x, preferred_element_type=F32)
                cr, ci = halves(v[:128, :128], v[:128, 128:])
                sr, si = halves(v[128:, :128], v[128:, 128:])
                if s == 0:
                    re = jnp.concatenate([cr[:32] + keep * si[:32], cr[32:] + si[32:], ci[:32]], axis=0)
                    im = jnp.concatenate([keep * ci[:32] - sr[:32], ci[32:] - sr[32:], -si[:32]], axis=0)
                else:
                    re, im = cr + si, ci - sr
                z.append((re, im))
            (ar, ai), (br, bi), (cr, ci), (dr, di) = z
            sr, si, tr, ti = ar + cr, ai + ci, br + dr, bi + di
            er, ei, fr, fi = ar - cr, ai - ci, br - dr, bi - di
            lanes = pl.ds(pl.multiple_of(128 * q, 128), 128)
            for ref, re, im in (
                (u0, sr + tr, si + ti),
                (u1, er + fi, ei - fr),
                (u2, sr - tr, si - ti),
                (u3, er - fi, ei + fr),
            ):
                ref[:count, lanes] = re.astype(BF16)
                ref[count : 2 * count, lanes] = im.astype(BF16)
            return carry

        lax.fori_loop(0, 4, time_step, 0)

        def products(ref, table):
            both = jnp.dot(ref[: 2 * count], table, preferred_element_type=F32)
            return both[:count, :128], both[:count, 128:], both[count:, :128], both[count:, 128:]

        def put(member, quarter, value):
            blocks[s, member, :, 128 * quarter : 128 * (quarter + 1)] = value.astype(BF16)

        def mirrored(value):
            if s == 1:
                return value
            return jnp.concatenate([jnp.where(special, value[128:], value[:32]), value[32:128]], axis=0)

        def odd_step(b):
            up = plus(*products(u1, ty[2, b]))
            put(b, 1, up[:128])
            put(7 - b, 3, mirrored(up))
            down = minus(*products(u3, ty[2, b]))
            put(4 + b, 1, mirrored(down))
            put(3 - b, 3, down[:128])

        def even_step(b):
            for c, ref in ((0, u0), (2, u2)):
                parts = products(ref, ty[c // 2, b])
                put(b, c, plus(*parts)[:128])
                put(4 + b, c, mirrored(minus(*parts)))

        def pair_step(i, carry):
            low = (i + my_core) & 1
            far = jnp.where(a >> 1 == 0, 3 - low, low)
            for b in (far, 3 - far):
                odd_step(b)
                even_step(b)

            def pieces(n, carry):
                to = jnp.where(n & 3 < 2, 3 - far, far)
                send_piece(s, to + TA * ((n + 1) & 1), n >> 2)
                return carry

            lax.fori_loop(0, 4 * (128 // PIECE), pieces, 0)
            return carry

        lax.fori_loop(0, 2, pair_step, 0)
        if s == 0:

            @pl.when(part == 0)
            def _():
                for ta in range(TA):
                    pltpu.make_async_remote_copy(
                        src_ref=blocks.at[0, 4 + ta, pl.ds(0, FR)], dst_ref=corner_out,
                        send_sem=corner_send, recv_sem=corner_recv, device_id=(ta, corner_to), device_id_type=MESH,
                    ).start()

    @pl.when(part == 0)
    def _():
        all_corners = blocks.at[0, 0]
        pltpu.make_async_copy(all_corners, all_corners, corner_send).wait()

    @pl.when(h == 1)
    def _():
        pltpu.make_async_copy(corner_out, corner_out, corner_recv).wait()

    for s in range(2):
        pltpu.make_async_copy(most, most, send).wait()
    pltpu.make_async_copy(out.at[0], out.at[0], local2).wait()
    seven = out.at[pl.ds(0, 7)]
    pltpu.make_async_copy(seven, seven, recv2).wait()
    pltpu.make_async_copy(seven, seven, send2).wait()


def fused(field, xt, tt, ty, scale):
    anywhere = pl.BlockSpec(memory_space=pl.ANY)
    operands = (field, xt, tt, ty)
    dma = pltpu.SemaphoreType.DMA
    return pl.pallas_call(
        functools.partial(fused_kernel, scale),
        out_shape=(
            jax.ShapeDtypeStruct((8, 256, 512), BF16),
            jax.ShapeDtypeStruct((FR, 512), BF16),
        ),
        in_specs=[anywhere] * 4,
        out_specs=(anywhere, anywhere),
        scratch_shapes=[pltpu.VMEM(x.shape, BF16) for x in operands]
        + [pltpu.VMEM((2, FT * YL, NX // 2), BF16)]
        + [pltpu.VMEM((2, DEV, 4 * FT, 128), BF16)] * 2
        + [pltpu.VMEM((320, 512), BF16)] * 4
        + [pltpu.VMEM((2, 8, 128, 512), BF16)]
        + [dma((FT,)), dma((2, CHUNKS)), dma((2,)), dma, dma((2,)), dma((2,))]
        + [dma] * 5,
        compiler_params=pltpu.CompilerParams(collective_id=3, has_side_effects=True, vmem_limit_bytes=56 * MIB),
        name="fused",
    )(*operands)


LAST_STEPS = 2
LAST = 8 // LAST_STEPS


def last_kernel(blocks, corner, rows, order, out, turned, below):
    mirrored = lax.axis_index("gy") >= HALF
    rows_here = rows[jnp.where(mirrored, 1, 0)]
    first = (lax.broadcasted_iota(jnp.int32, (8 * FR, 512), 0) % 8 == 0) & mirrored

    @pl.when(pl.program_id(0) == 0)
    def _():
        edge = jnp.concatenate([corner[...], jnp.zeros((7 * FR, 512), BF16)], axis=0)
        below[...] = jnp.dot(rows_here, edge, preferred_element_type=F32)

    for m in range(LAST):
        here = jnp.dot(rows_here, blocks[m], preferred_element_type=F32)
        turned[m] = jnp.where(first, below[...], here).astype(BF16)
        below[...] = here
    for n in range(2):
        lanes = slice(256 * n, 256 * (n + 1))
        all_rows = turned[...].reshape(LAST * 8 * FR, 512)
        done = jnp.dot(all_rows, order[:, lanes], preferred_element_type=F32).reshape(LAST, FR, 8, 256)
        for m in range(LAST):
            out[:, 8 * m : 8 * m + 8, lanes] = done[m]


def last_step(blocks, corner, rows, order):
    return pl.pallas_call(
        last_kernel,
        grid=(LAST_STEPS,),
        out_shape=jax.ShapeDtypeStruct((FR, 64, 512), F32),
        in_specs=[
            pl.BlockSpec((LAST, 256, 512), lambda m: (m, 0, 0)),
            pl.BlockSpec((FR, 512), lambda m: (0, 0)),
            pl.BlockSpec((2, 256, 256), lambda m: (0, 0, 0)),
            pl.BlockSpec((512, 512), lambda m: (0, 0)),
        ],
        out_specs=pl.BlockSpec((FR, 8 * LAST, 512), lambda m: (0, m, 0)),
        scratch_shapes=[pltpu.VMEM((LAST, 8 * FR, 512), BF16), pltpu.VMEM((8 * FR, 512), F32)],
        compiler_params=pltpu.CompilerParams(vmem_limit_bytes=62 * MIB),
        name="last_step",
    )(blocks, corner, rows, order)


def shards(charge_field):
    tt, wsum = t_table()
    tables = [jnp.asarray(x) for x in (x_tables(), tt, y_tables())]
    blocks, corner = fused(charge_field, *tables, 1.0 / (NX * NY * wsum))
    return last_step(blocks, corner, jnp.asarray(row_tables()), jnp.asarray(ky_table()))


def solution(mesh):
    return jax.shard_map(
        shards, mesh=mesh, in_specs=(P("ta", "gy", None),), out_specs=P(None, "gy", "ta"), check_vma=False
    )
```

```python
import functools
import math

import jax
import jax.numpy as jnp
import ml_dtypes
import numpy as np
from jax import lax
from jax.experimental import pallas as pl
from jax.experimental.pallas import tpu as pltpu
from jax.sharding import PartitionSpec as P

FR, NX, NY = 32, 2048, 2048
TA, GY = 4, 32
DEV = TA * GY
FT = FR // TA
YL = NY // GY
SLOT = 8
HALF = GY // 2
F32, BF16 = jnp.float32, jnp.bfloat16
MIB = 1 << 20


def bf(a):
    return np.asarray(a).astype(np.float32).astype(ml_dtypes.bfloat16)


def place(group, part):
    a, h = part % TA, part // TA
    return a, group if h == 0 else GY - 1 - group


def order_of(a, g):
    y, core = 2 * (a // 2) + g // 16, a % 2
    z, x = g // 4 % 4, g % 4
    return ((x + y + z) % 4 * 2 + core) * 16 + 4 * y + x


@functools.lru_cache(None)
def x_tables():
    kx = np.zeros((2, DEV, 4), np.int64)
    for group in range(HALF):
        for part in range(8):
            for parity in range(2):
                base = 64 * group + 8 * part + parity
                kx[parity, order_of(*place(group, part))] = base + 2 * np.arange(4)
    n = np.arange(NX // 2)
    angle = 2 * np.pi * ((kx[..., None] * n) % NX) / NX
    re, im = np.cos(angle), -np.sin(angle)
    zero = order_of(*place(0, 0))
    im[0, zero, 0] = np.cos(np.pi * n)
    both = np.stack([re, im], axis=2)
    return bf(both.reshape(2, DEV * 8, NX // 2))


@functools.lru_cache(None)
def t_table():
    t = np.arange(FR)
    window = 0.5 - 0.5 * np.cos(2 * np.pi * (t + 0.5) / FR)
    angle = 2 * np.pi * ((t[:, None] * t[None, :]) % FR) / FR
    out = np.zeros((2, 4, FR, FR, 4))
    for p in range(4):
        out[0, p, :, :, p] = np.cos(angle) * window
        out[1, p, :, :, p] = np.sin(angle) * window
    return bf(out.reshape(2 * 4 * FR, FR * 4)), float(np.sum(window * window))


@functools.lru_cache(None)
def y_tables():
    n, k = np.arange(NY // 4), np.arange(NY // 4)
    out = []
    for q in (0, 2, 1):
        angle = 2 * np.pi * ((n[:, None] * (4 * k[None, :] + q)) % NY) / NY
        cs = np.stack([np.cos(angle).reshape(-1, 4, 128), np.sin(angle).reshape(-1, 4, 128)], axis=2)
        out.append(cs.transpose(1, 0, 2, 3).reshape(4, NY // 4, 256))
    return bf(np.stack(out))


@functools.lru_cache(None)
def row_tables():
    out = np.zeros((2, FR, 8, 2, 4, FR))
    for w in range(FR):
        for j in range(8):
            out[0, w, j, j % 2, j // 2, w] = 1
            out[1, w, (8 - j) % 8, j % 2, j // 2, -w % FR] = 1
    return bf(out.reshape(2, FR * 8, FR * 8))


@functools.lru_cache(None)
def ky_table():
    out = np.zeros((4, 128, 128, 4))
    k = np.arange(128)
    for q in range(3):
        out[q, k, k, q] = 1
    out[3, k, 127 - k, 3] = 1
    return bf(out.reshape(512, 512))


def halves(first, second):
    low = lax.broadcasted_iota(jnp.int32, first.shape, first.ndim - 1) < 64
    one = jnp.where(low, first, pltpu.roll(second, 64, first.ndim - 1))
    two = jnp.where(low, pltpu.roll(first, 64, first.ndim - 1), second)
    return one, two


NT = (((1,), (1,)), ((), ()))
MESH, LOGICAL = pl.DeviceIdType.MESH, pl.DeviceIdType.LOGICAL
CHUNKS = 8
CHUNK = DEV // CHUNKS
PIECE = 32


def fused_kernel(
    scale, field_in, xt_in, tt_in, ty_in, out, corner_out,
    field, xt, tt, ty, folded, slots, rec, u0, u1, u2, u3, blocks,
    frame_load, table_load, load, send, recv, local, send2, recv2, local2, corner_send, corner_recv,
):
    a, g = lax.axis_index("ta"), lax.axis_index("gy")
    me = a * GY + g
    my_y, my_core, my_z, my_x = 2 * (a >> 1) + (g >> 4), a & 1, (g >> 2) & 3, g & 3
    first = ((my_x + my_y + my_z) & 3) * 2 + my_core
    barrier = pltpu.get_barrier_semaphore()

    def frame(t):
        return pltpu.make_async_copy(field_in.at[t], field.at[t], frame_load.at[t])

    def table(s, c):
        rows = pl.ds(pl.multiple_of(128 * ((first + c) & 7), 128), 128)
        return pltpu.make_async_copy(xt_in.at[s, rows], xt.at[s, rows], table_load.at[s, c])

    loads = [pltpu.make_async_copy(src, dst, load.at[i]) for i, (src, dst) in enumerate(((tt_in, tt), (ty_in, ty)))]

    for t in range(FT):
        frame(t).start()
    table(0, 0).start()
    table(0, 1).start()

    for o in range(1, DEV):
        peer = (me + o) & (DEV - 1)
        pl.semaphore_signal(barrier, inc=1, device_id=peer, device_id_type=LOGICAL)

    for t in range(FT):
        frame(t).wait()
        rows = slice(YL * t, YL * (t + 1))
        lo = field[t, :, : NX // 2].astype(F32)
        hi = field[t, :, NX // 2 :].astype(F32)
        folded[0, rows] = (lo + hi).astype(BF16)
        folded[1, rows] = (lo - hi).astype(BF16)

    def x_step(s, c):
        table(s, c).wait()
        k = (first + c) & 7
        rows = pl.ds(pl.multiple_of(128 * k, 128), 128)
        tile = (16, 8, 128)
        stay = (lax.broadcasted_iota(jnp.int32, tile, 1) < 4) == (lax.broadcasted_iota(jnp.int32, tile, 2) < 64)
        for n in range(2):
            both = lax.dot_general(
                xt[s, rows], folded[s, 256 * n : 256 * (n + 1)], NT, preferred_element_type=F32
            )
            parts = []
            for q in range(2):
                part = both[:, 128 * q : 128 * (q + 1)].reshape(tile)
                parts.append(jnp.where(stay, part, pltpu.roll(pltpu.roll(part, 64, 2), 4, 1)))
            slots[s, pl.ds(16 * k, 16), 16 * n : 16 * (n + 1)] = jnp.concatenate(parts, axis=1).astype(BF16)

    def send_step(s, c):
        k = (first + c) & 7
        total, core = k >> 1, k & 1
        for i in range(CHUNK):
            y, x = (my_y + (i >> 2)) & 3, (my_x + i) & 3
            z = (total + 8 - x - y) & 3
            src = slots.at[s, 16 * k + 4 * y + x]
            dst = rec.at[s, me]
            if i == 0 and isinstance(c, int) and c == 0:
                pltpu.make_async_copy(src, dst, local.at[s]).start()
                continue
            pltpu.make_async_remote_copy(
                src_ref=src, dst_ref=dst, send_sem=send, recv_sem=recv.at[s],
                device_id=GY * (2 * (y >> 1) + core) + 16 * (y & 1) + 4 * z + x, device_id_type=LOGICAL,
            ).start()

    for s in range(2):
        x_step(s, 0)
        if s == 0:
            pl.semaphore_wait(barrier, DEV - 1)
        else:
            send_step(0, CHUNKS - 1)
        send_step(s, 0)
        if s == 0:
            for c in range(2, CHUNKS):
                table(0, c).start()
            for c in range(CHUNKS):
                table(1, c).start()
        x_step(s, 1)

        def step(c, carry):
            send_step(s, c - 1)
            x_step(s, c)
            return carry

        lax.fori_loop(2, CHUNKS, step, 0)
        if s == 0:
            for copy in loads:
                copy.start()
    send_step(1, CHUNKS - 1)

    for copy in loads:
        copy.wait()

    special = (a == 0) & (g == 0)
    keep = jnp.where(special, 0.0, 1.0).astype(F32)
    h = g >> 4
    group = jnp.where(h == 0, g, GY - 1 - g)
    part = a + TA * h

    def send_piece(s, member, piece):
        ta, th = member & 3, member >> 2
        tg = jnp.where(th == 0, group, GY - 1 - group)
        rows = pl.ds(pl.multiple_of(PIECE * piece, PIECE), PIECE)
        to_rows = pl.ds(pl.multiple_of(128 * s + PIECE * piece, PIECE), PIECE)
        src = blocks.at[s, member, rows]
        dst = out.at[jnp.where(th == 0, part, 7 - part), to_rows]

        @pl.when(member == part)
        def _():
            pltpu.make_async_copy(src, dst, local2).start()

        @pl.when(member != part)
        def _():
            pltpu.make_async_remote_copy(
                src_ref=src, dst_ref=dst, send_sem=send2, recv_sem=recv2, device_id=(ta, tg), device_id_type=MESH
            ).start()

    def plus(p1, p2, p3, p4):
        re, im = p1 + p4, p3 - p2
        return (re * re + im * im) * scale

    def minus(p1, p2, p3, p4):
        re, im = p1 - p4, p3 + p2
        return (re * re + im * im) * scale

    most = rec.at[0, pl.ds(0, DEV - 1)]
    corner_to = GY - 1 - ((group + HALF - 1) & (HALF - 1))

    for s in range(2):
        count = 160 if s == 0 else 128
        pltpu.make_async_copy(slots.at[s, 0], rec.at[s, 0], local.at[s]).wait()
        pltpu.make_async_copy(most, most, recv.at[s]).wait()

        def rec_of(row):
            return jnp.concatenate([rec[s, GY * t + row] for t in range(TA)], axis=0)

        def time_step(q, carry):
            z = []
            for n in range(4):
                pair = 4 * n + q
                x = jnp.concatenate([rec_of(2 * pair), rec_of(2 * pair + 1)], axis=1)
                v = jnp.dot(tt[...], x, preferred_element_type=F32)
                cr, ci = halves(v[:128, :128], v[:128, 128:])
                sr, si = halves(v[128:, :128], v[128:, 128:])
                if s == 0:
                    re = jnp.concatenate([cr[:32] + keep * si[:32], cr[32:] + si[32:], ci[:32]], axis=0)
                    im = jnp.concatenate([keep * ci[:32] - sr[:32], ci[32:] - sr[32:], -si[:32]], axis=0)
                else:
                    re, im = cr + si, ci - sr
                z.append((re, im))
            (ar, ai), (br, bi), (cr, ci), (dr, di) = z
            sr, si, tr, ti = ar + cr, ai + ci, br + dr, bi + di
            er, ei, fr, fi = ar - cr, ai - ci, br - dr, bi - di
            lanes = pl.ds(pl.multiple_of(128 * q, 128), 128)
            for ref, re, im in (
                (u0, sr + tr, si + ti),
                (u1, er + fi, ei - fr),
                (u2, sr - tr, si - ti),
                (u3, er - fi, ei + fr),
            ):
                ref[:count, lanes] = re.astype(BF16)
                ref[count : 2 * count, lanes] = im.astype(BF16)
            return carry

        lax.fori_loop(0, 4, time_step, 0)

        def products(ref, table):
            both = jnp.dot(ref[: 2 * count], table, preferred_element_type=F32)
            return both[:count, :128], both[:count, 128:], both[count:, :128], both[count:, 128:]

        def put(member, quarter, value):
            blocks[s, member, :, 128 * quarter : 128 * (quarter + 1)] = value.astype(BF16)

        def mirrored(value):
            if s == 1:
                return value
            return jnp.concatenate([jnp.where(special, value[128:], value[:32]), value[32:128]], axis=0)

        def odd_step(b):
            up = plus(*products(u1, ty[2, b]))
            put(b, 1, up[:128])
            put(7 - b, 3, mirrored(up))
            down = minus(*products(u3, ty[2, b]))
            put(4 + b, 1, mirrored(down))
            put(3 - b, 3, down[:128])

        def even_step(b):
            for c, ref in ((0, u0), (2, u2)):
                parts = products(ref, ty[c // 2, b])
                put(b, c, plus(*parts)[:128])
                put(4 + b, c, mirrored(minus(*parts)))

        def pair_step(i, carry):
            low = (i + my_core) & 1
            far = jnp.where(a >> 1 == 0, 3 - low, low)
            for b in (far, 3 - far):
                odd_step(b)
                even_step(b)

            def pieces(n, carry):
                to = jnp.where(n & 3 < 2, 3 - far, far)
                send_piece(s, to + TA * ((n + 1) & 1), n >> 2)
                return carry

            lax.fori_loop(0, 4 * (128 // PIECE), pieces, 0)
            return carry

        lax.fori_loop(0, 2, pair_step, 0)
        if s == 0:

            @pl.when(part == 0)
            def _():
                for ta in range(TA):
                    pltpu.make_async_remote_copy(
                        src_ref=blocks.at[0, 4 + ta, pl.ds(0, FR)], dst_ref=corner_out,
                        send_sem=corner_send, recv_sem=corner_recv, device_id=(ta, corner_to), device_id_type=MESH,
                    ).start()

    @pl.when(part == 0)
    def _():
        all_corners = blocks.at[0, 0]
        pltpu.make_async_copy(all_corners, all_corners, corner_send).wait()

    @pl.when(h == 1)
    def _():
        pltpu.make_async_copy(corner_out, corner_out, corner_recv).wait()

    for s in range(2):
        pltpu.make_async_copy(most, most, send).wait()
    pltpu.make_async_copy(out.at[0], out.at[0], local2).wait()
    seven = out.at[pl.ds(0, 7)]
    pltpu.make_async_copy(seven, seven, recv2).wait()
    pltpu.make_async_copy(seven, seven, send2).wait()


def fused(field, xt, tt, ty, scale):
    anywhere = pl.BlockSpec(memory_space=pl.ANY)
    operands = (field, xt, tt, ty)
    dma = pltpu.SemaphoreType.DMA
    return pl.pallas_call(
        functools.partial(fused_kernel, scale),
        out_shape=(
            jax.ShapeDtypeStruct((8, 256, 512), BF16),
            jax.ShapeDtypeStruct((FR, 512), BF16),
        ),
        in_specs=[anywhere] * 4,
        out_specs=(anywhere, anywhere),
        scratch_shapes=[pltpu.VMEM(x.shape, BF16) for x in operands]
        + [pltpu.VMEM((2, FT * YL, NX // 2), BF16)]
        + [pltpu.VMEM((2, DEV, 4 * FT, 128), BF16)] * 2
        + [pltpu.VMEM((320, 512), BF16)] * 4
        + [pltpu.VMEM((2, 8, 128, 512), BF16)]
        + [dma((FT,)), dma((2, CHUNKS)), dma((2,)), dma, dma((2,)), dma((2,))]
        + [dma] * 5,
        compiler_params=pltpu.CompilerParams(collective_id=3, has_side_effects=True, vmem_limit_bytes=56 * MIB),
        name="fused",
    )(*operands)


LAST_STEPS = 2
LAST = 8 // LAST_STEPS


def last_kernel(blocks, corner, rows, order, out, turned, below):
    mirrored = lax.axis_index("gy") >= HALF
    rows_here = rows[0]
    first = (lax.broadcasted_iota(jnp.int32, (8 * FR, 512), 0) % 8 == 0) & mirrored

    @pl.when(pl.program_id(0) == 0)
    def _():
        edge = jnp.concatenate([corner[...], jnp.zeros((7 * FR, 512), BF16)], axis=0)
        below[...] = jnp.dot(rows_here, edge, preferred_element_type=F32)

    for m in range(LAST):
        here = jnp.dot(rows_here, blocks[m], preferred_element_type=F32)
        turned[m] = jnp.where(first, below[...], here).astype(BF16)
        below[...] = here
    for n in range(2):
        lanes = slice(256 * n, 256 * (n + 1))
        all_rows = turned[...].reshape(LAST * 8 * FR, 512)
        done = jnp.dot(all_rows, order[:, lanes], preferred_element_type=F32).reshape(LAST, FR, 8, 256)
        for m in range(LAST):
            out[:, 8 * m : 8 * m + 8, lanes] = done[m]


def last_step(blocks, corner, rows, order):
    return pl.pallas_call(
        last_kernel,
        grid=(LAST_STEPS,),
        out_shape=jax.ShapeDtypeStruct((FR, 64, 512), F32),
        in_specs=[
            pl.BlockSpec((LAST, 256, 512), lambda m: (m, 0, 0)),
            pl.BlockSpec((FR, 512), lambda m: (0, 0)),
            pl.BlockSpec((1, 256, 256), lambda m: (lax.axis_index("gy") // HALF, 0, 0)),
            pl.BlockSpec((512, 512), lambda m: (0, 0)),
        ],
        out_specs=pl.BlockSpec((FR, 8 * LAST, 512), lambda m: (0, m, 0)),
        scratch_shapes=[pltpu.VMEM((LAST, 8 * FR, 512), BF16), pltpu.VMEM((8 * FR, 512), F32)],
        compiler_params=pltpu.CompilerParams(vmem_limit_bytes=62 * MIB),
        name="last_step",
    )(blocks, corner, rows, order)


def shards(charge_field):
    tt, wsum = t_table()
    tables = [jnp.asarray(x) for x in (x_tables(), tt, y_tables())]
    blocks, corner = fused(charge_field, *tables, 1.0 / (NX * NY * wsum))
    return last_step(blocks, corner, jnp.asarray(row_tables()), jnp.asarray(ky_table()))


def solution(mesh):
    return jax.shard_map(
        shards, mesh=mesh, in_specs=(P("ta", "gy", None),), out_specs=P(None, "gy", "ta"), check_vma=False
    )
```

```python
import functools
import math

import jax
import jax.numpy as jnp
import ml_dtypes
import numpy as np
from jax import lax
from jax.experimental import pallas as pl
from jax.experimental.pallas import tpu as pltpu
from jax.sharding import PartitionSpec as P

FR, NX, NY = 32, 2048, 2048
TA, GY = 4, 32
DEV = TA * GY
FT = FR // TA
YL = NY // GY
SLOT = 8
HALF = GY // 2
F32, BF16 = jnp.float32, jnp.bfloat16
MIB = 1 << 20


def bf(a):
    return np.asarray(a).astype(np.float32).astype(ml_dtypes.bfloat16)


def place(group, part):
    a, h = part % TA, part // TA
    return a, group if h == 0 else GY - 1 - group


def order_of(a, g):
    y, core = 2 * (a // 2) + g // 16, a % 2
    z, x = g // 4 % 4, g % 4
    return ((x + y + z) % 4 * 2 + core) * 16 + 4 * y + x


@functools.lru_cache(None)
def x_tables():
    kx = np.zeros((2, DEV, 4), np.int64)
    for group in range(HALF):
        for part in range(8):
            for parity in range(2):
                base = 64 * group + 8 * part + parity
                kx[parity, order_of(*place(group, part))] = base + 2 * np.arange(4)
    n = np.arange(NX // 2)
    angle = 2 * np.pi * ((kx[..., None] * n) % NX) / NX
    re, im = np.cos(angle), -np.sin(angle)
    zero = order_of(*place(0, 0))
    im[0, zero, 0] = np.cos(np.pi * n)
    both = np.stack([re, im], axis=2)
    return bf(both.reshape(2, DEV * 8, NX // 2))


@functools.lru_cache(None)
def t_table():
    t = np.arange(FR)
    window = 0.5 - 0.5 * np.cos(2 * np.pi * (t + 0.5) / FR)
    angle = 2 * np.pi * ((t[:, None] * t[None, :]) % FR) / FR
    out = np.zeros((2, 4, FR, FR, 4))
    for p in range(4):
        out[0, p, :, :, p] = np.cos(angle) * window
        out[1, p, :, :, p] = np.sin(angle) * window
    return bf(out.reshape(2 * 4 * FR, FR * 4)), float(np.sum(window * window))


@functools.lru_cache(None)
def y_tables():
    n, k = np.arange(NY // 4), np.arange(NY // 4)
    out = []
    for q in (0, 2, 1):
        angle = 2 * np.pi * ((n[:, None] * (4 * k[None, :] + q)) % NY) / NY
        cs = np.stack([np.cos(angle).reshape(-1, 4, 128), np.sin(angle).reshape(-1, 4, 128)], axis=2)
        out.append(cs.transpose(1, 0, 2, 3).reshape(4, NY // 4, 256))
    return bf(np.stack(out))


@functools.lru_cache(None)
def row_tables():
    out = np.zeros((2, FR, 8, 2, 4, FR))
    for w in range(FR):
        for j in range(8):
            out[0, w, j, j % 2, j // 2, w] = 1
            out[1, w, (8 - j) % 8, j % 2, j // 2, -w % FR] = 1
    return bf(out.reshape(2, FR * 8, FR * 8))


@functools.lru_cache(None)
def ky_table():
    out = np.zeros((4, 128, 128, 4))
    k = np.arange(128)
    for q in range(3):
        out[q, k, k, q] = 1
    out[3, k, 127 - k, 3] = 1
    return bf(out.reshape(512, 512))


def halves(first, second):
    low = lax.broadcasted_iota(jnp.int32, first.shape, first.ndim - 1) < 64
    one = jnp.where(low, first, pltpu.roll(second, 64, first.ndim - 1))
    two = jnp.where(low, pltpu.roll(first, 64, first.ndim - 1), second)
    return one, two


NT = (((1,), (1,)), ((), ()))
MESH = pl.DeviceIdType.MESH
CHUNKS = 8
CHUNK = DEV // CHUNKS
PIECE = 32


def fused_kernel(
    scale, field_in, xt_in, tt_in, ty_in, out, corner_out,
    field, xt, tt, ty, folded, slots, rec, u0, u1, u2, u3, blocks,
    frame_load, table_load, load, send, recv, local, send2, recv2, local2, corner_send, corner_recv,
):
    a, g = lax.axis_index("ta"), lax.axis_index("gy")
    me = a * GY + g
    my_y, my_core, my_z, my_x = 2 * (a >> 1) + (g >> 4), a & 1, (g >> 2) & 3, g & 3
    first = ((my_x + my_y + my_z) & 3) * 2 + my_core
    barrier = pltpu.get_barrier_semaphore()

    def frame(t):
        return pltpu.make_async_copy(field_in.at[t], field.at[t], frame_load.at[t])

    def table(s, c):
        rows = pl.ds(pl.multiple_of(128 * ((first + c) & 7), 128), 128)
        return pltpu.make_async_copy(xt_in.at[s, rows], xt.at[s, rows], table_load.at[s, c])

    loads = [pltpu.make_async_copy(src, dst, load.at[i]) for i, (src, dst) in enumerate(((tt_in, tt), (ty_in, ty)))]

    for t in range(FT):
        frame(t).start()
    table(0, 0).start()
    table(0, 1).start()

    for o in range(1, DEV):
        peer = (me + o) & (DEV - 1)
        pl.semaphore_signal(barrier, inc=1, device_id=(peer >> 5, peer & 31), device_id_type=MESH)

    for t in range(FT):
        frame(t).wait()
        rows = slice(YL * t, YL * (t + 1))
        lo = field[t, :, : NX // 2].astype(F32)
        hi = field[t, :, NX // 2 :].astype(F32)
        folded[0, rows] = (lo + hi).astype(BF16)
        folded[1, rows] = (lo - hi).astype(BF16)

    def x_step(s, c):
        table(s, c).wait()
        k = (first + c) & 7
        rows = pl.ds(pl.multiple_of(128 * k, 128), 128)
        tile = (16, 8, 128)
        stay = (lax.broadcasted_iota(jnp.int32, tile, 1) < 4) == (lax.broadcasted_iota(jnp.int32, tile, 2) < 64)
        for n in range(2):
            both = lax.dot_general(
                xt[s, rows], folded[s, 256 * n : 256 * (n + 1)], NT, preferred_element_type=F32
            )
            parts = []
            for q in range(2):
                part = both[:, 128 * q : 128 * (q + 1)].reshape(tile)
                parts.append(jnp.where(stay, part, pltpu.roll(pltpu.roll(part, 64, 2), 4, 1)))
            slots[s, pl.ds(16 * k, 16), 16 * n : 16 * (n + 1)] = jnp.concatenate(parts, axis=1).astype(BF16)

    def send_step(s, c):
        k = (first + c) & 7
        total, core = k >> 1, k & 1
        for i in range(CHUNK):
            y, x = (my_y + (i >> 2)) & 3, (my_x + 3 * i) & 3
            z = (total + 8 - x - y) & 3
            src = slots.at[s, 16 * k + 4 * y + x]
            dst = rec.at[s, me]
            if i == 0 and isinstance(c, int) and c == 0:
                pltpu.make_async_copy(src, dst, local.at[s]).start()
                continue
            pltpu.make_async_remote_copy(
                src_ref=src, dst_ref=dst, send_sem=send, recv_sem=recv.at[s],
                device_id=(2 * (y >> 1) + core, 16 * (y & 1) + 4 * z + x), device_id_type=MESH,
            ).start()

    for s in range(2):
        x_step(s, 0)
        if s == 0:
            pl.semaphore_wait(barrier, DEV - 1)
        else:
            send_step(0, CHUNKS - 1)
        send_step(s, 0)
        if s == 0:
            for c in range(2, CHUNKS):
                table(0, c).start()
            for c in range(CHUNKS):
                table(1, c).start()
        x_step(s, 1)

        def step(c, carry):
            send_step(s, c - 1)
            x_step(s, c)
            return carry

        lax.fori_loop(2, CHUNKS, step, 0)
        if s == 0:
            for copy in loads:
                copy.start()
    send_step(1, CHUNKS - 1)

    for copy in loads:
        copy.wait()

    special = (a == 0) & (g == 0)
    keep = jnp.where(special, 0.0, 1.0).astype(F32)
    h = g >> 4
    group = jnp.where(h == 0, g, GY - 1 - g)
    part = a + TA * h

    def send_piece(s, member, piece):
        ta, th = member & 3, member >> 2
        tg = jnp.where(th == 0, group, GY - 1 - group)
        rows = pl.ds(pl.multiple_of(PIECE * piece, PIECE), PIECE)
        to_rows = pl.ds(pl.multiple_of(128 * s + PIECE * piece, PIECE), PIECE)
        src = blocks.at[s, member, rows]
        dst = out.at[jnp.where(th == 0, part, 7 - part), to_rows]

        @pl.when(member == part)
        def _():
            pltpu.make_async_copy(src, dst, local2).start()

        @pl.when(member != part)
        def _():
            pltpu.make_async_remote_copy(
                src_ref=src, dst_ref=dst, send_sem=send2, recv_sem=recv2, device_id=(ta, tg), device_id_type=MESH
            ).start()

    def plus(p1, p2, p3, p4):
        re, im = p1 + p4, p3 - p2
        return (re * re + im * im) * scale

    def minus(p1, p2, p3, p4):
        re, im = p1 - p4, p3 + p2
        return (re * re + im * im) * scale

    most = rec.at[0, pl.ds(0, DEV - 1)]
    corner_to = GY - 1 - ((group + HALF - 1) & (HALF - 1))

    for s in range(2):
        count = 160 if s == 0 else 128
        pltpu.make_async_copy(slots.at[s, 0], rec.at[s, 0], local.at[s]).wait()
        pltpu.make_async_copy(most, most, recv.at[s]).wait()

        def rec_of(row):
            return jnp.concatenate([rec[s, GY * t + row] for t in range(TA)], axis=0)

        def time_step(q, carry):
            z = []
            for n in range(4):
                pair = 4 * n + q
                x = jnp.concatenate([rec_of(2 * pair), rec_of(2 * pair + 1)], axis=1)
                v = jnp.dot(tt[...], x, preferred_element_type=F32)
                cr, ci = halves(v[:128, :128], v[:128, 128:])
                sr, si = halves(v[128:, :128], v[128:, 128:])
                if s == 0:
                    re = jnp.concatenate([cr[:32] + keep * si[:32], cr[32:] + si[32:], ci[:32]], axis=0)
                    im = jnp.concatenate([keep * ci[:32] - sr[:32], ci[32:] - sr[32:], -si[:32]], axis=0)
                else:
                    re, im = cr + si, ci - sr
                z.append((re, im))
            (ar, ai), (br, bi), (cr, ci), (dr, di) = z
            sr, si, tr, ti = ar + cr, ai + ci, br + dr, bi + di
            er, ei, fr, fi = ar - cr, ai - ci, br - dr, bi - di
            lanes = pl.ds(pl.multiple_of(128 * q, 128), 128)
            for ref, re, im in (
                (u0, sr + tr, si + ti),
                (u1, er + fi, ei - fr),
                (u2, sr - tr, si - ti),
                (u3, er - fi, ei + fr),
            ):
                ref[:count, lanes] = re.astype(BF16)
                ref[count : 2 * count, lanes] = im.astype(BF16)
            return carry

        lax.fori_loop(0, 4, time_step, 0)

        def products(ref, table):
            both = jnp.dot(ref[: 2 * count], table, preferred_element_type=F32)
            return both[:count, :128], both[:count, 128:], both[count:, :128], both[count:, 128:]

        def put(member, quarter, value):
            blocks[s, member, :, 128 * quarter : 128 * (quarter + 1)] = value.astype(BF16)

        def mirrored(value):
            if s == 1:
                return value
            return jnp.concatenate([jnp.where(special, value[128:], value[:32]), value[32:128]], axis=0)

        def odd_step(b):
            up = plus(*products(u1, ty[2, b]))
            put(b, 1, up[:128])
            put(7 - b, 3, mirrored(up))
            down = minus(*products(u3, ty[2, b]))
            put(4 + b, 1, mirrored(down))
            put(3 - b, 3, down[:128])

        def even_step(b):
            for c, ref in ((0, u0), (2, u2)):
                parts = products(ref, ty[c // 2, b])
                put(b, c, plus(*parts)[:128])
                put(4 + b, c, mirrored(minus(*parts)))

        def pair_step(i, carry):
            low = (i + my_core) & 1
            far = jnp.where(a >> 1 == 0, 3 - low, low)
            for b in (far, 3 - far):
                odd_step(b)
                even_step(b)

            def pieces(n, carry):
                to = jnp.where(n & 1 == 0, 3 - far, far)
                send_piece(s, to + TA * (1 - ((n >> 1) & 1)), n >> 2)
                return carry

            lax.fori_loop(0, 4 * (128 // PIECE), pieces, 0)
            return carry

        lax.fori_loop(0, 2, pair_step, 0)
        if s == 0:

            @pl.when(part == 0)
            def _():
                for ta in range(TA):
                    pltpu.make_async_remote_copy(
                        src_ref=blocks.at[0, 4 + ta, pl.ds(0, FR)], dst_ref=corner_out,
                        send_sem=corner_send, recv_sem=corner_recv, device_id=(ta, corner_to), device_id_type=MESH,
                    ).start()

    @pl.when(part == 0)
    def _():
        all_corners = blocks.at[0, 0]
        pltpu.make_async_copy(all_corners, all_corners, corner_send).wait()

    @pl.when(h == 1)
    def _():
        pltpu.make_async_copy(corner_out, corner_out, corner_recv).wait()

    for s in range(2):
        pltpu.make_async_copy(most, most, send).wait()
    pltpu.make_async_copy(out.at[0], out.at[0], local2).wait()
    seven = out.at[pl.ds(0, 7)]
    pltpu.make_async_copy(seven, seven, recv2).wait()
    pltpu.make_async_copy(seven, seven, send2).wait()


def fused(field, xt, tt, ty, scale):
    anywhere = pl.BlockSpec(memory_space=pl.ANY)
    operands = (field, xt, tt, ty)
    dma = pltpu.SemaphoreType.DMA
    return pl.pallas_call(
        functools.partial(fused_kernel, scale),
        out_shape=(
            jax.ShapeDtypeStruct((8, 256, 512), BF16),
            jax.ShapeDtypeStruct((FR, 512), BF16),
        ),
        in_specs=[anywhere] * 4,
        out_specs=(anywhere, anywhere),
        scratch_shapes=[pltpu.VMEM(x.shape, BF16) for x in operands]
        + [pltpu.VMEM((2, FT * YL, NX // 2), BF16)]
        + [pltpu.VMEM((2, DEV, 4 * FT, 128), BF16)] * 2
        + [pltpu.VMEM((320, 512), BF16)] * 4
        + [pltpu.VMEM((2, 8, 128, 512), BF16)]
        + [dma((FT,)), dma((2, CHUNKS)), dma((2,)), dma, dma((2,)), dma((2,))]
        + [dma] * 5,
        compiler_params=pltpu.CompilerParams(collective_id=3, has_side_effects=True, vmem_limit_bytes=56 * MIB),
        name="fused",
    )(*operands)


LAST_STEPS = 2
LAST = 8 // LAST_STEPS


def last_kernel(blocks, corner, rows, order, out, turned, below):
    mirrored = lax.axis_index("gy") >= HALF
    rows_here = rows[jnp.where(mirrored, 1, 0)]
    first = (lax.broadcasted_iota(jnp.int32, (8 * FR, 512), 0) % 8 == 0) & mirrored

    @pl.when(pl.program_id(0) == 0)
    def _():
        edge = jnp.concatenate([corner[...], jnp.zeros((7 * FR, 512), BF16)], axis=0)
        below[...] = jnp.dot(rows_here, edge, preferred_element_type=F32)

    for m in range(LAST):
        here = jnp.dot(rows_here, blocks[m], preferred_element_type=F32)
        turned[m] = jnp.where(first, below[...], here).astype(BF16)
        below[...] = here
    for n in range(2):
        lanes = slice(256 * n, 256 * (n + 1))
        all_rows = turned[...].reshape(LAST * 8 * FR, 512)
        done = jnp.dot(all_rows, order[:, lanes], preferred_element_type=F32).reshape(LAST, FR, 8, 256)
        for m in range(LAST):
            out[:, 8 * m : 8 * m + 8, lanes] = done[m]


def last_step(blocks, corner, rows, order):
    return pl.pallas_call(
        last_kernel,
        grid=(LAST_STEPS,),
        out_shape=jax.ShapeDtypeStruct((FR, 64, 512), F32),
        in_specs=[
            pl.BlockSpec((LAST, 256, 512), lambda m: (m, 0, 0)),
            pl.BlockSpec((FR, 512), lambda m: (0, 0)),
            pl.BlockSpec((2, 256, 256), lambda m: (0, 0, 0)),
            pl.BlockSpec((512, 512), lambda m: (0, 0)),
        ],
        out_specs=pl.BlockSpec((FR, 8 * LAST, 512), lambda m: (0, m, 0)),
        scratch_shapes=[pltpu.VMEM((LAST, 8 * FR, 512), BF16), pltpu.VMEM((8 * FR, 512), F32)],
        compiler_params=pltpu.CompilerParams(vmem_limit_bytes=62 * MIB),
        name="last_step",
    )(blocks, corner, rows, order)


def shards(charge_field):
    tt, wsum = t_table()
    tables = [jnp.asarray(x) for x in (x_tables(), tt, y_tables())]
    blocks, corner = fused(charge_field, *tables, 1.0 / (NX * NY * wsum))
    return last_step(blocks, corner, jnp.asarray(row_tables()), jnp.asarray(ky_table()))


def solution(mesh):
    return jax.shard_map(
        shards, mesh=mesh, in_specs=(P("ta", "gy", None),), out_specs=P(None, "gy", "ta"), check_vma=False
    )
```
